32 devices in a mesh: band: 2 (over y), bl: 4 (over z), dir: 2 (over x), pol: 2 (over core).
Axes of the slice: x: 2, y: 2, z: 4, core: 2. Of those that a mesh axis runs over, the one named last changes fastest.
Arguments:
- visibilities: float32 [8, 4, 2, 32, 2, 4096], P('band', 'bl', 'pol'), parts along dimension 0, may hold values from -6 to 6
- hour_angle: float32 [4, 2, 32], P(None, 'pol'), may hold values from -1.5 to 1.5
- antenna_layout_coords: float32 [2, 2048], replicated, may hold values from -4 to 4
- point_coords: float32 [2, 2, 512], replicated, may hold values from -1 to 1
- point_flux: float32 [2, 512], replicated, may hold values from 0.01 to 0.1
- counts: int32 [2], replicated, may hold values from 128 to 512, as said below
- peel_order: int32 [2], replicated, may hold values from 0 to 1, each once
- earlier_gain_amplitude: float32 [4, 2048], P('band'), parts along dimension 0, may hold values from 0.5 to 1.5
- earlier_gain_phase: float32 [4, 2048], P('band'), parts along dimension 0, may hold values from -3.140625 to 3.140625
- tile_blocks: int32 [4, 2], P('bl'), may hold values from 0 to 31, as said below
Outputs:
- residual: float32 [8, 4, 2, 32, 2, 4096], P('band', 'bl', 'pol', 'dir'), parts along dimension 0
The draws below stay inside these ranges and needn't reach their ends.
There are 2 independent parts, one for each index of `band`. The reference program is written for one: setup_inputs(seed, part) draws one part's arguments, and reference() takes and returns one part's arrays. A program takes and returns all parts, laid end to end along the dimension named above; an argument that names none is the same for every part. Nothing has to cross between parts.
Inputs may be any that keep to these rules, and one draw needn't show every extreme that they name: `tile_blocks`: each tile pairs two different antenna blocks. `counts`: one direction uses all 512 components.
All inputs are finite; a program needn't handle non-finite values.
Results may differ from the reference program's by a relative error of at most 0.002.
Values sent between devices are 32-bit elements; how exact they have to be, the bound alone decides.
A program may use at most 128 MiB of HBM per device.

```python
import math
import jax
import jax.numpy as jnp
from jax import lax

ARRAY_ANTENNAS = 2048
ABLK = 64
NAB = 32
COMP = 512
ITERS = 3
TPOL = 32
INTERVALS = 4
NT = 4
TIMES = 64
PEEL_DIRECTIONS = 2
N_POL = 2


def draw_tile_blocks(key, part):
    key = jax.random.fold_in(key, 11)
    left_key, right_key = jax.random.split(key)
    left_block = jax.random.randint(left_key, (NT, 1), 0, NAB)
    offset_value = jax.random.randint(right_key, (NT, 1), 1, NAB)
    right_block = (left_block + offset_value) % NAB
    return jnp.concatenate([left_block, right_block], axis=1).astype(jnp.int32)


def draw_counts(key, part):
    key = jax.random.fold_in(key, 13)
    value_key, place_key = jax.random.split(key)
    values = jax.random.randint(value_key, (PEEL_DIRECTIONS,), COMP // 4, COMP)
    fullest = jax.random.randint(place_key, (), 0, PEEL_DIRECTIONS)
    places = jnp.arange(PEEL_DIRECTIONS, dtype=jnp.int32)
    return jnp.where(places == fullest, COMP, values).astype(jnp.int32)


def block_levels(own_key, shape, pieces, low, top_value):
    factor_of, own = 1.0, jax.random.fold_in(own_key, 6)
    for dim, shards_of in pieces:
        heights = jnp.exp(jax.random.uniform(jax.random.fold_in(own, dim), (shards_of,), jnp.float32, low / len(pieces), top_value / len(pieces)))
        factor_of = factor_of * jnp.repeat(heights, shape[dim] // shards_of).reshape([-1 if axis == dim else 1 for axis in range(len(shape))])
    return factor_of


def gaussian(key, dims, width, most, cuts=(), kind=jnp.bfloat16):
    factor_of = block_levels(key, dims, cuts, -0.22, 0.18) if cuts else 1.0
    result = jax.random.normal(key, dims, jnp.float32) * width * factor_of
    return jnp.minimum(jnp.maximum(result, -most), most).astype(kind)


def setup_inputs(seed: int = 0, part: int = 0) -> dict:
    streams_of = jax.random.split(jax.random.key(seed), 11)
    part_splits = jax.random.split(jax.random.fold_in(streams_of[10], part), 11)
    return {
        "visibilities": gaussian(part_splits[0], (INTERVALS, NT, N_POL, TPOL, 2, ABLK * ABLK), 1.0, 6.0, ((1, 4), (2, 2)), jnp.float32),
        "hour_angle": jnp.clip(jax.random.uniform(streams_of[1], (INTERVALS, N_POL, TPOL), jnp.float32, -1.5, 1.5) * block_levels(streams_of[1], (INTERVALS, N_POL, TPOL), ((1, 2),), -0.4, 0.0), -1.5, 1.5),
        "antenna_layout_coords": gaussian(streams_of[2], (2, ARRAY_ANTENNAS), 1.0, 4.0, (), jnp.float32),
        "point_coords": jnp.clip(jax.random.uniform(streams_of[3], (PEEL_DIRECTIONS, 2, COMP), jnp.float32, -1.0, 1.0), -1.0, 1.0),
        "point_flux": jnp.clip(jnp.exp(jax.random.uniform(streams_of[4], (PEEL_DIRECTIONS, COMP), jnp.float32, math.log(0.01), math.log(0.1))), 0.01, 0.1),
        "counts": draw_counts(jax.random.fold_in(streams_of[10], 71), part),
        "peel_order": jax.random.permutation(streams_of[6], PEEL_DIRECTIONS).astype(jnp.int32),
        "earlier_gain_amplitude": jnp.clip(1.0 + 0.1 * jax.random.normal(part_splits[7], (PEEL_DIRECTIONS, ARRAY_ANTENNAS), jnp.float32), 0.5, 1.5),
        "earlier_gain_phase": jnp.clip(jax.random.uniform(part_splits[8], (PEEL_DIRECTIONS, ARRAY_ANTENNAS), jnp.float32, -3.140625, 3.140625), -3.140625, 3.140625),
        "tile_blocks": draw_tile_blocks(jax.random.fold_in(streams_of[10], 71), part),
    }


LAMBDA = 1.0
TWO_PI = 6.283185307179586


def select_blocks(values, onehot):
    blocks = onehot.shape[1]
    grouped = values.reshape(values.shape[:-1] + (blocks, values.shape[-1] // blocks))
    return jnp.einsum("kn,...np->...kp", onehot, grouped, precision=lax.Precision.HIGHEST)


def phasors(positions, hour_values, coords):
    hour_cosine = jnp.cos(hour_values)[:, None, :, None]
    hour_sine = jnp.sin(hour_values)[:, None, :, None]
    east_pos = positions[0][None, :, None, :]
    north_pos = positions[1][None, :, None, :]
    coord_u = east_pos * hour_cosine - north_pos * hour_sine
    coord_v = east_pos * hour_sine + north_pos * hour_cosine
    phase_angle = TWO_PI * (coord_u[..., None] * coords[0] + coord_v[..., None] * coords[1])
    return jnp.cos(phase_angle), jnp.sin(phase_angle)


def rounded_copy(values):
    rounded = values.astype(jnp.bfloat16)
    return lax.optimization_barrier(rounded).astype(jnp.float32)


def predict(left_pos, right_pos, hour_values, coords, weight):
    cos_left, sin_left = phasors(left_pos, hour_values, coords)
    cos_right, sin_right = phasors(right_pos, hour_values, coords)
    left_real_component = rounded_copy(cos_left)
    left_imag = rounded_copy(sin_left)
    stacked_right = jnp.concatenate([rounded_copy(cos_right * weight), rounded_copy(sin_right * weight)], axis=-1)
    real_left = jnp.concatenate([left_real_component, left_imag], axis=-1)
    left_imag_component = jnp.concatenate([left_imag, -left_real_component], axis=-1)
    einsum_form = "bktpc,bktqc->bktpq"
    model_real = jnp.einsum(einsum_form, real_left, stacked_right, precision=lax.Precision.HIGHEST)
    model_imag = jnp.einsum(einsum_form, left_imag_component, stacked_right, precision=lax.Precision.HIGHEST)
    full_shape = model_real.shape
    flat_shape = full_shape[:3] + (full_shape[3] * full_shape[4],)
    return model_real.reshape(flat_shape), model_imag.reshape(flat_shape)


def outer_gains(left_real_component, left_imag, right_real, right_imag):
    outer_real = left_real_component[..., :, None] * right_real[..., None, :] + left_imag[..., :, None] * right_imag[..., None, :]
    outer_imag = left_imag[..., :, None] * right_real[..., None, :] - left_real_component[..., :, None] * right_imag[..., None, :]
    merged_shape = outer_real.shape[:-2] + (outer_real.shape[-2] * outer_real.shape[-1],)
    return outer_real.reshape(merged_shape), outer_imag.reshape(merged_shape)


def peel_update(current, model_real, model_imag, prior_real, prior_imag, left_hot, right_hot, total_fn):
    highest = lax.Precision.HIGHEST
    prior_outer = outer_gains(select_blocks(prior_real, left_hot), select_blocks(prior_imag, left_hot),
                              select_blocks(prior_real, right_hot), select_blocks(prior_imag, right_hot))
    outer_real = prior_outer[0][None, :, None, :]
    outer_imag = prior_outer[1][None, :, None, :]
    work_real = current[:, :, :, 0] + (outer_real * model_real - outer_imag * model_imag)
    work_imag = current[:, :, :, 1] + (outer_real * model_imag + outer_imag * model_real)
    batch_size = model_real.shape[0]
    tile_count = model_real.shape[1]
    tile_block_width = prior_real.shape[0] // left_hot.shape[1]
    square = (batch_size, tile_count, tile_block_width, tile_block_width)
    cross_real = jnp.sum(work_real * model_real + work_imag * model_imag, axis=2).reshape(square)
    cross_imag = jnp.sum(work_imag * model_real - work_real * model_imag, axis=2).reshape(square)
    model_power = jnp.sum(model_real * model_real + model_imag * model_imag, axis=2).reshape(square)
    gain_real = jnp.ones((batch_size, prior_real.shape[0]), jnp.float32)
    gain_imag = jnp.zeros((batch_size, prior_real.shape[0]), jnp.float32)
    row_form = "bkpq,bkq->bkp"
    column_form = "bkpq,bkp->bkq"
    for iteration in range(ITERS):
        left_real_component = select_blocks(gain_real, left_hot)
        left_imag = select_blocks(gain_imag, left_hot)
        right_real = select_blocks(gain_real, right_hot)
        right_imag = select_blocks(gain_imag, right_hot)
        left_terms = jnp.stack([
            jnp.einsum(row_form, cross_real, right_real, precision=highest) - jnp.einsum(row_form, cross_imag, right_imag, precision=highest),
            jnp.einsum(row_form, cross_real, right_imag, precision=highest) + jnp.einsum(row_form, cross_imag, right_real, precision=highest),
            jnp.einsum(row_form, model_power, right_real * right_real + right_imag * right_imag, precision=highest)], axis=1)
        right_terms = jnp.stack([
            jnp.einsum(column_form, cross_real, left_real_component, precision=highest) + jnp.einsum(column_form, cross_imag, left_imag, precision=highest),
            jnp.einsum(column_form, cross_real, left_imag, precision=highest) - jnp.einsum(column_form, cross_imag, left_real_component, precision=highest),
            jnp.einsum(column_form, model_power, left_real_component * left_real_component + left_imag * left_imag, precision=highest)], axis=1)
        normals = jnp.einsum("kn,bxkp->bxnp", left_hot, left_terms, precision=highest) + jnp.einsum("kn,bxkp->bxnp", right_hot, right_terms, precision=highest)
        normals = total_fn(normals.reshape(batch_size, 3, prior_real.shape[0]))
        new_real = (normals[:, 0] + LAMBDA * gain_real) / (normals[:, 2] + LAMBDA)
        new_imag = (normals[:, 1] + LAMBDA * gain_imag) / (normals[:, 2] + LAMBDA)
        gain_real = 0.5 * (gain_real + new_real)
        gain_imag = 0.5 * (gain_imag + new_imag)
    final_outer = outer_gains(select_blocks(gain_real, left_hot), select_blocks(gain_imag, left_hot),
                              select_blocks(gain_real, right_hot), select_blocks(gain_imag, right_hot))
    fitted_real = final_outer[0][:, :, None, :]
    fitted_imag = final_outer[1][:, :, None, :]
    out_real = work_real - (fitted_real * model_real - fitted_imag * model_imag)
    out_imag = work_imag - (fitted_real * model_imag + fitted_imag * model_real)
    return jnp.stack([out_real, out_imag], axis=3)


def keep_total(normals):
    return normals


def reference(visibilities, hour_angle, antenna_layout_coords, point_coords, point_flux, counts, peel_order, earlier_gain_amplitude, earlier_gain_phase, tile_blocks):
    tile_block_width = ABLK
    hour_values = hour_angle.reshape(INTERVALS, TIMES)
    residual_state = visibilities.reshape(INTERVALS, NT, TIMES, 2, tile_block_width * tile_block_width)
    block_ids = jnp.arange(NAB, dtype=jnp.int32)[None, :]
    left_hot = (tile_blocks[:, 0:1] == block_ids).astype(jnp.float32)
    right_hot = (tile_blocks[:, 1:2] == block_ids).astype(jnp.float32)
    left_pos = jnp.moveaxis(select_blocks(antenna_layout_coords, left_hot), 1, 0)
    right_pos = jnp.moveaxis(select_blocks(antenna_layout_coords, right_hot), 1, 0)
    point_index = jnp.arange(COMP, dtype=jnp.int32)

    def one_section(position, current):
        direction = lax.dynamic_index_in_dim(peel_order, position, 0, keepdims=False)
        coords = lax.dynamic_index_in_dim(point_coords, direction, 0, keepdims=False)
        live_count = lax.dynamic_index_in_dim(counts, direction, 0, keepdims=False)
        weight = lax.dynamic_index_in_dim(point_flux, direction, 0, keepdims=False) * (point_index < live_count).astype(jnp.float32)

        def one_tile(tile_pair):
            model_real, model_imag = predict(tile_pair[0][:, None, :], tile_pair[1][:, None, :], hour_values, coords, weight)
            return model_real[:, 0], model_imag[:, 0]

        model_real, model_imag = lax.map(one_tile, (left_pos, right_pos))
        model_real = jnp.transpose(model_real, (1, 0, 2, 3))
        model_imag = jnp.transpose(model_imag, (1, 0, 2, 3))
        amplitude = lax.dynamic_index_in_dim(earlier_gain_amplitude, direction, 0, keepdims=False)
        prior_angle = lax.dynamic_index_in_dim(earlier_gain_phase, direction, 0, keepdims=False)
        return peel_update(current, model_real, model_imag, amplitude * jnp.cos(prior_angle), amplitude * jnp.sin(prior_angle), left_hot, right_hot, keep_total)

    residual_state = lax.fori_loop(0, PEEL_DIRECTIONS, one_section, residual_state)
    return residual_state.reshape(INTERVALS, NT, N_POL, TPOL, 2, tile_block_width * tile_block_width)
```

```python
import functools

import jax
import jax.numpy as jnp
from jax import lax
from jax.experimental import pallas as pl
from jax.experimental.pallas import tpu as pltpu
from jax.sharding import PartitionSpec as P

ABLK = 64
ITERS = 3
LAMBDA = 1.0
HALF = ABLK // 2
LANES = 2 * ABLK
CHUNK = 128
MESH = pl.DeviceIdType.MESH
HIGHEST = lax.Precision.HIGHEST
SIN_C = (4.442867911308811, -7.307443741853454, 3.5947910749268956, -0.784381842458349)
COS_C = (1.4142040873683897, -6.977642700991201, 5.715246760161864, -1.7283748369726175)


def half_turns(turns):
    part = turns - jnp.round(turns)
    square = part * part
    sine = SIN_C[-1]
    for value in SIN_C[-2::-1]:
        sine = sine * square + value
    cosine = COS_C[-1]
    for value in COS_C[-2::-1]:
        cosine = cosine * square + value
    return part * sine, cosine


def swap_halves(values):
    return pltpu.roll(values, ABLK, 1)


def predict_sample(chunks, pos_ref, east_row, north_row, weight_row):
    left_cos, left_sin, right_cos, right_sin = [], [], [], []
    for chunk in range(chunks):
        lanes = slice(chunk * CHUNK, (chunk + 1) * CHUNK)
        east, north, weight = east_row[:, lanes], north_row[:, lanes], weight_row[:, lanes]
        sine, cosine = half_turns(pos_ref[0] * east + pos_ref[1] * north)
        left_cos.append((1.0 - sine * sine).astype(jnp.bfloat16))
        left_sin.append((sine * cosine).astype(jnp.bfloat16))
        sine, cosine = half_turns(pos_ref[2] * east + pos_ref[3] * north)
        weighted = sine * weight
        right_cos.append((weight - weighted * sine).astype(jnp.bfloat16))
        right_sin.append((weighted * cosine).astype(jnp.bfloat16))
    left = jnp.concatenate(
        [jnp.concatenate(left_cos, axis=1), jnp.concatenate(left_sin, axis=1)], axis=0
    )
    right = jnp.concatenate(
        [jnp.concatenate(right_cos, axis=1), jnp.concatenate(right_sin, axis=1)], axis=0
    )
    out = lax.dot_general(
        left, right, (((1,), (1,)), ((), ())), preferred_element_type=jnp.float32
    )
    cos_even, cos_odd = out[:HALF], out[HALF:ABLK]
    sin_even, sin_odd = out[ABLK : ABLK + HALF], out[ABLK + HALF :]
    first = lax.broadcasted_iota(jnp.int32, (HALF, LANES), 1) < ABLK
    real = jnp.where(first, cos_even, swap_halves(cos_odd)) + jnp.where(
        first, swap_halves(sin_even), sin_odd
    )
    imag = jnp.where(first, sin_even, swap_halves(sin_odd)) - jnp.where(
        first, swap_halves(cos_even), cos_odd
    )
    return real, imag


def model_kernel(
    sections,
    times,
    comps,
    unroll,
    scalars,
    pos_ref,
    east_ref,
    north_ref,
    weight_ref,
    prior_ref,
    vis_ref,
    model_ref,
    sums_ref,
):
    def one_section(section):
        weight_row = weight_ref[section]

        def run(chunks):
            def sample(time, carry):
                real, imag = predict_sample(
                    chunks,
                    pos_ref,
                    east_ref[0, section, pl.ds(time, 1), :],
                    north_ref[0, section, pl.ds(time, 1), :],
                    weight_row,
                )
                model_ref[0, section, time, 0] = real
                model_ref[0, section, time, 1] = imag
                return carry

            lax.fori_loop(0, times, sample, 0, unroll=unroll)

        for chunks in range(1, comps // CHUNK + 1):
            pl.when(scalars[1 + section] == chunks)(functools.partial(run, chunks))

    if sections <= 2:
        for section in range(sections):
            one_section(section)
    else:
        lax.fori_loop(0, sections, lambda s, c: (one_section(s), c)[1], 0)

    zero = jnp.zeros((HALF, LANES), jnp.float32)
    pair = 3 * sections
    for section in range(sections):

        def with_vis(time, carry):
            cross_real, cross_imag, power = carry
            real, imag = model_ref[0, section, time, 0], model_ref[0, section, time, 1]
            vis_real = vis_ref[0, time, pl.ds(0, HALF, 2), :]
            vis_imag = vis_ref[0, time, pl.ds(1, HALF, 2), :]
            return (
                cross_real + (vis_real * real + vis_imag * imag),
                cross_imag + (vis_imag * real - vis_real * imag),
                power + (real * real + imag * imag),
            )

        cross_real, cross_imag, power = lax.fori_loop(0, times, with_vis, (zero, zero, zero))
        cross_real += prior_ref[section, 0] * power
        cross_imag += prior_ref[section, 1] * power
        for other in range(section):

            def with_model(time, carry):
                pair_real, pair_imag = carry
                real, imag = model_ref[0, section, time, 0], model_ref[0, section, time, 1]
                other_real, other_imag = model_ref[0, other, time, 0], model_ref[0, other, time, 1]
                return (
                    pair_real + (other_real * real + other_imag * imag),
                    pair_imag + (other_imag * real - other_real * imag),
                )

            pair_real, pair_imag = lax.fori_loop(0, times, with_model, (zero, zero))
            prior_real, prior_imag = prior_ref[other, 0], prior_ref[other, 1]
            cross_real += prior_real * pair_real - prior_imag * pair_imag
            cross_imag += prior_real * pair_imag + prior_imag * pair_real
            sums_ref[0, pl.ds(pair * HALF, HALF), :] = pair_real
            sums_ref[0, pl.ds((pair + 1) * HALF, HALF), :] = pair_imag
            pair += 2
        sums_ref[0, pl.ds(3 * section * HALF, HALF), :] = cross_real
        sums_ref[0, pl.ds((3 * section + 1) * HALF, HALF), :] = cross_imag
        sums_ref[0, pl.ds((3 * section + 2) * HALF, HALF), :] = power


def each(count, body):
    if count <= 4:
        for index in range(count):
            body(index)
    else:
        lax.fori_loop(0, count, lambda index, carry: (body(index), carry)[1], 0)


def solve_kernel(
    sections,
    intervals,
    tiles,
    dirs,
    pols,
    sums_ref,
    ids_ref,
    out_ref,
    part_ref,
    tile_ref,
    gain_msg_ref,
    square_ref,
    gain_ref,
    normal_ref,
    final_ref,
    part_send,
    part_recv,
    tile_send,
    tile_recv,
    gain_send,
    gain_recv,
):
    group = dirs * pols
    rows = sums_ref.shape[1]
    here = lax.axis_index("bl")
    me = lax.axis_index("dir") * pols + lax.axis_index("pol")

    def group_peer(step):
        peer = lax.rem(me + step, group)
        return peer, {"dir": peer // pols, "pol": lax.rem(peer, pols)}

    barrier = pltpu.get_barrier_semaphore()
    for step in range(1, group):
        pl.semaphore_signal(barrier, inc=1, device_id=group_peer(step)[1], device_id_type=MESH)
    for step in range(1, tiles):
        pl.semaphore_signal(
            barrier, inc=1, device_id={"bl": lax.rem(here + step, tiles)}, device_id_type=MESH
        )
    pl.semaphore_wait(barrier, group - 1 + tiles - 1)

    copies = []
    for step in range(1, group):
        peer, where = group_peer(step)
        copies.append(
            pltpu.make_async_remote_copy(
                src_ref=sums_ref.at[lax.rem(peer, intervals)],
                dst_ref=part_ref.at[step - 1],
                send_sem=part_send.at[step - 1],
                recv_sem=part_recv.at[step - 1],
                device_id=where,
                device_id_type=MESH,
            )
        )
        copies[-1].start()
    total = sums_ref[lax.rem(me, intervals)]
    for step in range(1, group):
        copies[step - 1].wait_recv()
        total += part_ref[step - 1]
    tile_ref[here, pl.ds(0, rows), :] = total
    tile_ref[here, pl.ds(rows, 8), :] = ids_ref[...]
    for copy in copies:
        copy.wait_send()

    copies = []
    for step in range(1, tiles):
        copies.append(
            pltpu.make_async_remote_copy(
                src_ref=tile_ref.at[here],
                dst_ref=tile_ref.at[here],
                send_sem=tile_send.at[step - 1],
                recv_sem=tile_recv.at[step - 1],
                device_id={"bl": lax.rem(here + step, tiles)},
                device_id_type=MESH,
            )
        )
        copies[-1].start()
    for copy in copies:
        copy.wait()

    sides = 2 * tiles
    ids = jnp.concatenate(
        [tile_ref[k, pl.ds(rows, 1), :] for k in range(tiles)]
        + [tile_ref[k, pl.ds(rows + 1, 1), :] for k in range(tiles)],
        axis=0,
    )[:, :ABLK]

    def shared_sum(values):
        total = jnp.zeros((sides, ABLK), jnp.float32)
        for side in range(sides):
            total += jnp.where(ids == ids[side : side + 1], values[side : side + 1], 0.0)
        return total

    def unpack(tile, slot, index):
        packed = tile_ref[tile, pl.ds(index * HALF, HALF), :]
        square_ref[tile, slot, pl.ds(0, HALF, 2), :] = packed
        square_ref[tile, slot, pl.ds(1, HALF, 2), :] = swap_halves(packed)

    def side_rows(real, imag):
        return jnp.concatenate(
            [real, imag, real * real + imag * imag, jnp.zeros((5, ABLK), jnp.float32)], axis=0
        )

    pair = 3 * sections
    for section in range(sections):

        def load_tile(tile):
            for slot in range(3):
                unpack(tile, slot, 3 * section + slot)

        each(tiles, load_tile)
        for other in range(section):

            def take_off(tile, other=other, pair=pair):
                unpack(tile, 3, pair)
                unpack(tile, 4, pair + 1)
                left_real = final_ref[other, 0, pl.ds(tile, 1), :]
                left_imag = final_ref[other, 1, pl.ds(tile, 1), :]
                right_real = final_ref[other, 0, pl.ds(tiles + tile, 1), :]
                right_imag = final_ref[other, 1, pl.ds(tiles + tile, 1), :]
                tall = jnp.concatenate(
                    [left_real, left_imag, jnp.zeros((6, ABLK), jnp.float32)], axis=0
                )
                zeros = jnp.zeros((6, ABLK), jnp.float32)
                form = (((0,), (0,)), ((), ()))
                outer_real = lax.dot_general(
                    tall,
                    jnp.concatenate([right_real, right_imag, zeros], axis=0),
                    form,
                    precision=HIGHEST,
                    preferred_element_type=jnp.float32,
                )
                outer_imag = lax.dot_general(
                    tall,
                    jnp.concatenate([-right_imag, right_real, zeros], axis=0),
                    form,
                    precision=HIGHEST,
                    preferred_element_type=jnp.float32,
                )
                pair_real = square_ref[tile, 3, :, pl.ds(0, ABLK)]
                pair_imag = square_ref[tile, 4, :, pl.ds(0, ABLK)]
                square_ref[tile, 0, :, pl.ds(0, ABLK)] -= (
                    outer_real * pair_real - outer_imag * pair_imag
                )
                square_ref[tile, 1, :, pl.ds(0, ABLK)] -= (
                    outer_real * pair_imag + outer_imag * pair_real
                )

            each(tiles, take_off)
            pair += 2

        gain_ref[0] = jnp.ones((sides, ABLK), jnp.float32)
        gain_ref[1] = jnp.zeros((sides, ABLK), jnp.float32)
        for _ in range(ITERS):

            def tile_normals(tile):
                cross_real = square_ref[tile, 0, :, pl.ds(0, ABLK)]
                cross_imag = square_ref[tile, 1, :, pl.ds(0, ABLK)]
                power = square_ref[tile, 2, :, pl.ds(0, ABLK)]
                from_right = side_rows(
                    gain_ref[0, pl.ds(tiles + tile, 1), :], gain_ref[1, pl.ds(tiles + tile, 1), :]
                )
                from_left = side_rows(
                    gain_ref[0, pl.ds(tile, 1), :], gain_ref[1, pl.ds(tile, 1), :]
                )

                def along(values, matrix, dim):
                    return lax.dot_general(
                        values,
                        matrix,
                        (((1,), (dim,)), ((), ())),
                        precision=HIGHEST,
                        preferred_element_type=jnp.float32,
                    )

                by_real, by_imag = along(from_right, cross_real, 1), along(from_right, cross_imag, 1)
                normal_ref[0, pl.ds(tile, 1), :] = by_real[0:1] - by_imag[1:2]
                normal_ref[1, pl.ds(tile, 1), :] = by_real[1:2] + by_imag[0:1]
                normal_ref[2, pl.ds(tile, 1), :] = along(from_right, power, 1)[2:3]
                by_real, by_imag = along(from_left, cross_real, 0), along(from_left, cross_imag, 0)
                normal_ref[0, pl.ds(tiles + tile, 1), :] = by_real[0:1] + by_imag[1:2]
                normal_ref[1, pl.ds(tiles + tile, 1), :] = by_real[1:2] - by_imag[0:1]
                normal_ref[2, pl.ds(tiles + tile, 1), :] = along(from_left, power, 0)[2:3]

            each(tiles, tile_normals)
            gain_real, gain_imag = gain_ref[0], gain_ref[1]
            below = shared_sum(normal_ref[2]) + LAMBDA
            gain_ref[0] = 0.5 * (
                gain_real + (shared_sum(normal_ref[0]) + LAMBDA * gain_real) / below
            )
            gain_ref[1] = 0.5 * (
                gain_imag + (shared_sum(normal_ref[1]) + LAMBDA * gain_imag) / below
            )
        final_ref[section] = gain_ref[...]

    for section in range(sections):
        for row, (kind, side) in enumerate(((0, here), (1, here), (0, tiles + here), (1, tiles + here))):
            gain_msg_ref[me, section, pl.ds(row, 1), pl.ds(0, ABLK)] = final_ref[
                section, kind, pl.ds(side, 1), :
            ]
    copies = []
    for step in range(1, group):
        copies.append(
            pltpu.make_async_remote_copy(
                src_ref=gain_msg_ref.at[me],
                dst_ref=gain_msg_ref.at[me],
                send_sem=gain_send.at[step - 1],
                recv_sem=gain_recv.at[step - 1],
                device_id=group_peer(step)[1],
                device_id_type=MESH,
            )
        )
        copies[-1].start()
    for copy in copies:
        copy.wait()
    for interval in range(intervals):
        out_ref[interval] = gain_msg_ref[interval, :, pl.ds(0, 4), pl.ds(0, ABLK)]


def residual_kernel(sections, times, scalars, vis_ref, model_ref, factor_ref, out_ref):
    def sample(time, carry):
        real = vis_ref[0, time, pl.ds(0, HALF, 2), :]
        imag = vis_ref[0, time, pl.ds(1, HALF, 2), :]
        for section in range(sections):
            model_real = model_ref[0, section, time, 0]
            model_imag = model_ref[0, section, time, 1]
            factor_real, factor_imag = factor_ref[0, section, 0], factor_ref[0, section, 1]
            real += factor_real * model_real - factor_imag * model_imag
            imag += factor_real * model_imag + factor_imag * model_real
        out_ref[0, time, pl.ds(0, HALF, 2), :] = real
        out_ref[0, time, pl.ds(1, HALF, 2), :] = imag
        return carry

    lax.fori_loop(0, times, sample, 0)


def outer_gains(left_real, left_imag, right_real, right_imag):
    real = left_real[..., :, None] * right_real[..., None, :] + (
        left_imag[..., :, None] * right_imag[..., None, :]
    )
    imag = left_imag[..., :, None] * right_real[..., None, :] - (
        left_real[..., :, None] * right_imag[..., None, :]
    )
    both = jnp.stack([real, imag], axis=-3)
    return both.reshape(both.shape[:-2] + (HALF, LANES))


def on_device(
    visibilities,
    hour_angle,
    antenna_layout_coords,
    point_coords,
    point_flux,
    counts,
    peel_order,
    earlier_gain_amplitude,
    earlier_gain_phase,
    tile_blocks,
):
    sections, dirs = point_coords.shape[0], lax.axis_size("dir")
    pols, tiles = lax.axis_size("pol"), lax.axis_size("bl")
    group = dirs * pols
    comps = point_flux.shape[1]
    intervals, total_times = visibilities.shape[0], visibilities.shape[3]
    times = total_times // dirs
    me_dir = lax.axis_index("dir")
    assert group % intervals == 0 and group >= intervals

    vis = visibilities.reshape(intervals, total_times, 2, HALF, LANES)
    vis = vis.transpose(0, 1, 3, 2, 4).reshape(intervals, total_times, ABLK, LANES)
    hours = lax.dynamic_slice_in_dim(hour_angle[:, 0], me_dir * times, times, 1)
    hour_cos, hour_sin = jnp.cos(hours)[..., None], jnp.sin(hours)[..., None]
    coords = point_coords[peel_order]
    live = counts[peel_order]
    weight = point_flux[peel_order] * (jnp.arange(comps)[None] < live[:, None]).astype(jnp.float32)
    l_row, m_row = coords[None, :, 0, None, :], coords[None, :, 1, None, :]
    hour_cos, hour_sin = hour_cos[:, None], hour_sin[:, None]
    east = l_row * hour_cos + m_row * hour_sin
    north = m_row * hour_cos - l_row * hour_sin
    chunks = jnp.clip((live + CHUNK - 1) // CHUNK, 1, comps // CHUNK)
    scalars = jnp.concatenate([me_dir[None], chunks]).astype(jnp.int32)

    left_block, right_block = tile_blocks[0, 0], tile_blocks[0, 1]

    def block_of(values, block):
        return lax.dynamic_slice_in_dim(values, block * ABLK, ABLK, values.ndim - 1)

    left_pos = block_of(antenna_layout_coords, left_block)
    left_pos = left_pos.reshape(2, HALF, 2).transpose(0, 2, 1).reshape(2, ABLK)
    positions = jnp.concatenate([left_pos, block_of(antenna_layout_coords, right_block)], axis=0)
    positions = jnp.broadcast_to(positions[:, :, None], (4, ABLK, CHUNK))
    prior_sides = []
    for block in (left_block, right_block):
        amplitude = block_of(earlier_gain_amplitude, block)[peel_order]
        angle = block_of(earlier_gain_phase, block)[peel_order]
        prior_sides += [amplitude * jnp.cos(angle), amplitude * jnp.sin(angle)]
    prior = outer_gains(*prior_sides)

    count = 3 * sections + sections * (sections - 1)
    rows = count * HALF
    whole = lambda shape: pl.BlockSpec(shape, lambda i, s: (0,) * len(shape))
    vis_spec = pl.BlockSpec((1, times, ABLK, LANES), lambda i, s: (i, s[0], 0, 0))
    model_spec = pl.BlockSpec(
        (1, sections, times, 2, HALF, LANES), lambda i, s: (i, 0, 0, 0, 0, 0)
    )
    row_spec = pl.BlockSpec((1, sections, times, comps), lambda i, s: (i, 0, 0, 0))
    limit = 48 * 1024 * 1024
    model, sums = pl.pallas_call(
        functools.partial(model_kernel, sections, times, comps, 2),
        out_shape=(
            jax.ShapeDtypeStruct((intervals, sections, times, 2, HALF, LANES), jnp.float32),
            jax.ShapeDtypeStruct((intervals, rows, LANES), jnp.float32),
        ),
        grid_spec=pltpu.PrefetchScalarGridSpec(
            num_scalar_prefetch=1,
            grid=(intervals,),
            in_specs=[
                whole((4, ABLK, CHUNK)),
                row_spec,
                row_spec,
                whole((sections, 1, comps)),
                whole((sections, 2, HALF, LANES)),
                vis_spec,
            ],
            out_specs=(
                model_spec,
                pl.BlockSpec((1, rows, LANES), lambda i, s: (i, 0, 0)),
            ),
        ),
        compiler_params=pltpu.CompilerParams(vmem_limit_bytes=limit),
        name="models",
    )(scalars, positions, east, north, weight[:, None], prior, vis)

    ids = jnp.concatenate([tile_blocks[0], jnp.zeros((6,), jnp.int32)]).astype(jnp.float32)
    ids = jnp.broadcast_to(ids[:, None], (8, LANES))
    vmem = pl.BlockSpec(memory_space=pltpu.VMEM)
    dma = pltpu.SemaphoreType.DMA
    gains = pl.pallas_call(
        functools.partial(solve_kernel, sections, intervals, tiles, dirs, pols),
        out_shape=jax.ShapeDtypeStruct((intervals, sections, 4, ABLK), jnp.float32),
        in_specs=[vmem, vmem],
        out_specs=vmem,
        scratch_shapes=[
            pltpu.VMEM((group - 1, rows, LANES), jnp.float32),
            pltpu.VMEM((tiles, rows + 8, LANES), jnp.float32),
            pltpu.VMEM((group, sections, 8, LANES), jnp.float32),
            pltpu.VMEM((tiles, 5, ABLK, LANES), jnp.float32),
            pltpu.VMEM((2, 2 * tiles, ABLK), jnp.float32),
            pltpu.VMEM((3, 2 * tiles, ABLK), jnp.float32),
            pltpu.VMEM((sections, 2, 2 * tiles, ABLK), jnp.float32),
            dma((group - 1,)),
            dma((group - 1,)),
            dma((tiles - 1,)),
            dma((tiles - 1,)),
            dma((group - 1,)),
            dma((group - 1,)),
        ],
        compiler_params=pltpu.CompilerParams(
            collective_id=0, has_side_effects=True, vmem_limit_bytes=56 * 1024 * 1024
        ),
        name="solve",
    )(sums, ids)

    factor = prior[None] - outer_gains(
        gains[:, :, 0], gains[:, :, 1], gains[:, :, 2], gains[:, :, 3]
    )
    out = pl.pallas_call(
        functools.partial(residual_kernel, sections, times),
        out_shape=jax.ShapeDtypeStruct((intervals, times, ABLK, LANES), jnp.float32),
        grid_spec=pltpu.PrefetchScalarGridSpec(
            num_scalar_prefetch=1,
            grid=(intervals,),
            in_specs=[
                vis_spec,
                model_spec,
                pl.BlockSpec((1, sections, 2, HALF, LANES), lambda i, s: (i, 0, 0, 0, 0)),
            ],
            out_specs=pl.BlockSpec((1, times, ABLK, LANES), lambda i, s: (i, 0, 0, 0)),
        ),
        compiler_params=pltpu.CompilerParams(vmem_limit_bytes=limit),
        name="residual",
    )(scalars, vis, model, factor)
    out = out.reshape(intervals, times, HALF, 2, LANES).transpose(0, 1, 3, 2, 4)
    return out.reshape(intervals, 1, 1, times, 2, HALF * LANES)


def solution(mesh):
    placed = (
        P("band", "bl", "pol", None, None, None),
        P(None, "pol", None),
        P(),
        P(),
        P(),
        P(),
        P(),
        P("band", None),
        P("band", None),
        P("bl", None),
    )
    return jax.shard_map(
        on_device,
        mesh=mesh,
        in_specs=placed,
        out_specs=P("band", "bl", "pol", "dir", None, None),
        check_vma=False,
    )
```

```python
import functools

import jax
import jax.numpy as jnp
from jax import lax
from jax.experimental import pallas as pl
from jax.experimental.pallas import tpu as pltpu
from jax.sharding import PartitionSpec as P

ABLK = 64
ITERS = 3
LAMBDA = 1.0
HALF = ABLK // 2
LANES = 2 * ABLK
CHUNK = 128
MESH = pl.DeviceIdType.MESH
SIN_C = (4.442867911308811, -7.307443741853454, 3.5947910749268956, -0.784381842458349)
COS_C = (1.4142040873683897, -6.977642700991201, 5.715246760161864, -1.7283748369726175)


def half_turns(turns):
    part = turns - jnp.round(turns)
    square = part * part
    sine = SIN_C[-1]
    for value in SIN_C[-2::-1]:
        sine = sine * square + value
    cosine = COS_C[-1]
    for value in COS_C[-2::-1]:
        cosine = cosine * square + value
    return part * sine, cosine


def swap_halves(values):
    return pltpu.roll(values, ABLK, 1)


def predict_sample(chunks, pos_ref, east_row, north_row, weight_row):
    left_cos, left_sin, right_cos, right_sin = [], [], [], []
    for chunk in range(chunks):
        lanes = slice(chunk * CHUNK, (chunk + 1) * CHUNK)
        east, north, weight = east_row[:, lanes], north_row[:, lanes], weight_row[:, lanes]
        sine, cosine = half_turns(pos_ref[0] * east + pos_ref[1] * north)
        left_cos.append((1.0 - sine * sine).astype(jnp.bfloat16))
        left_sin.append((sine * cosine).astype(jnp.bfloat16))
        sine, cosine = half_turns(pos_ref[2] * east + pos_ref[3] * north)
        weighted = sine * weight
        right_cos.append((weight - weighted * sine).astype(jnp.bfloat16))
        right_sin.append((weighted * cosine).astype(jnp.bfloat16))
    left = jnp.concatenate(
        [jnp.concatenate(left_cos, axis=1), jnp.concatenate(left_sin, axis=1)], axis=0
    )
    right = jnp.concatenate(
        [jnp.concatenate(right_cos, axis=1), jnp.concatenate(right_sin, axis=1)], axis=0
    )
    out = lax.dot_general(
        left, right, (((1,), (1,)), ((), ())), preferred_element_type=jnp.float32
    )
    cos_even, cos_odd = out[:HALF], out[HALF:ABLK]
    sin_even, sin_odd = out[ABLK : ABLK + HALF], out[ABLK + HALF :]
    first = lax.broadcasted_iota(jnp.int32, (HALF, LANES), 1) < ABLK
    real = jnp.where(first, cos_even, swap_halves(cos_odd)) + jnp.where(
        first, swap_halves(sin_even), sin_odd
    )
    imag = jnp.where(first, sin_even, swap_halves(sin_odd)) - jnp.where(
        first, swap_halves(cos_even), cos_odd
    )
    return real, imag


def columns(rows):
    count = len(rows)
    pad = jnp.zeros((8 - count, LANES), jnp.float32)
    turned = jnp.concatenate(list(rows) + [pad], axis=0).T
    return [jnp.broadcast_to(turned[:ABLK, k : k + 1], (ABLK, LANES)) for k in range(count)]


def both_halves(row):
    first = lax.broadcasted_iota(jnp.int32, (1, LANES), 1) < ABLK
    return jnp.where(first, row, swap_halves(row))


def outer_packed(left_real, left_imag, right_real, right_imag, column_ref):
    first = lax.broadcasted_iota(jnp.int32, (HALF, LANES), 1) < ABLK
    packed = []
    for slot, column in enumerate(columns([left_real, left_imag])):
        column_ref[slot] = column
        packed.append(
            jnp.where(
                first,
                column_ref[slot, pl.ds(0, HALF, 2), :],
                column_ref[slot, pl.ds(1, HALF, 2), :],
            )
        )
    real, imag = packed
    return real * right_real + imag * right_imag, imag * right_real - real * right_imag


def pick_row(values, row):
    here = lax.broadcasted_iota(jnp.int32, values.shape, 0) == row
    return jnp.sum(jnp.where(here, values, 0.0), axis=0, keepdims=True)


def block_row(ref, row, block):
    start = pl.multiple_of((block // 2) * LANES, LANES)
    both = pick_row(ref[:, pl.ds(start, LANES)], row)
    return jnp.where(lax.rem(block, 2) == 1, swap_halves(both), both)


def model_kernel(
    sections,
    times,
    comps,
    unroll,
    dir_ref,
    order_ref,
    counts_ref,
    blocks_ref,
    layout_ref,
    coords_ref,
    flux_ref,
    amplitude_ref,
    angle_ref,
    hour_ref,
    vis_ref,
    model_ref,
    sums_ref,
    prior_ref,
    pos_ref,
    weight_ref,
    column_ref,
    east_ref,
    north_ref,
):
    left_block, right_block = blocks_ref[0, 0], blocks_ref[0, 1]

    @pl.when(pl.program_id(0) == 0)
    def _():
        sides = columns(
            [
                block_row(layout_ref, 0, left_block),
                block_row(layout_ref, 1, left_block),
                block_row(layout_ref, 0, right_block),
                block_row(layout_ref, 1, right_block),
            ]
        )
        for slot in range(2):
            column_ref[slot] = sides[slot]
            pos_ref[slot, pl.ds(0, HALF), :] = column_ref[slot, pl.ds(0, HALF, 2), :]
            pos_ref[slot, pl.ds(HALF, HALF), :] = column_ref[slot, pl.ds(1, HALF, 2), :]
            pos_ref[2 + slot] = sides[2 + slot]
        for section in range(sections):
            direction = order_ref[section]
            live = lax.broadcasted_iota(jnp.int32, (1, comps), 1) < counts_ref[direction]
            weight_ref[section] = jnp.where(live, pick_row(flux_ref[...], direction), 0.0)
            rows = []
            for block in (left_block, right_block):
                amplitude = block_row(amplitude_ref, direction, block)
                angle = block_row(angle_ref, direction, block)
                rows += [amplitude * jnp.cos(angle), amplitude * jnp.sin(angle)]
            real, imag = outer_packed(
                rows[0], rows[1], both_halves(rows[2]), both_halves(rows[3]), column_ref
            )
            prior_ref[section, 0] = real
            prior_ref[section, 1] = imag

    hour_row = hour_ref[0]
    hour_row = jnp.concatenate(
        [hour_row, jnp.zeros((1, LANES - hour_row.shape[1]), jnp.float32)], axis=1
    )
    turned = jnp.concatenate(
        [jnp.cos(hour_row), jnp.sin(hour_row), jnp.zeros((6, LANES), jnp.float32)], axis=0
    ).T
    column_ref[0] = jnp.broadcast_to(turned[:ABLK, 0:1], (ABLK, LANES))
    column_ref[1] = jnp.broadcast_to(turned[:ABLK, 1:2], (ABLK, LANES))
    start = dir_ref[0] * times
    hour_cos = column_ref[0, pl.ds(start, times), :]
    hour_sin = column_ref[1, pl.ds(start, times), :]
    for section in range(sections):
        direction = order_ref[section]
        l_row, m_row = coords_ref[direction, 0:1, :], coords_ref[direction, 1:2, :]
        for chunk in range(comps // CHUNK):
            lanes = pl.ds(chunk * CHUNK, CHUNK)
            l_part = l_row[:, chunk * CHUNK : (chunk + 1) * CHUNK]
            m_part = m_row[:, chunk * CHUNK : (chunk + 1) * CHUNK]
            east_ref[section, :, lanes] = l_part * hour_cos + m_part * hour_sin
            north_ref[section, :, lanes] = m_part * hour_cos - l_part * hour_sin

    head_rows = 8
    side = lax.broadcasted_iota(jnp.int32, (head_rows, LANES), 0)
    sums_ref[0, pl.ds(0, head_rows), :] = jnp.where(
        side == 0, left_block, jnp.where(side == 1, right_block, 0)
    ).astype(jnp.float32)

    def one_section(section):
        weight_row = weight_ref[section]

        def run(chunks):
            def sample(time, carry):
                real, imag = predict_sample(
                    chunks,
                    pos_ref,
                    east_ref[section, pl.ds(time, 1), :],
                    north_ref[section, pl.ds(time, 1), :],
                    weight_row,
                )
                model_ref[0, section, time, 0] = real
                model_ref[0, section, time, 1] = imag
                return carry

            lax.fori_loop(0, times, sample, 0, unroll=unroll)

        most = comps // CHUNK
        needed = jnp.clip((counts_ref[order_ref[section]] + CHUNK - 1) // CHUNK, 1, most)
        for chunks in range(1, most + 1):
            pl.when(needed == chunks)(functools.partial(run, chunks))

    if sections <= 2:
        for section in range(sections):
            one_section(section)
    else:
        lax.fori_loop(0, sections, lambda s, c: (one_section(s), c)[1], 0)

    zero = jnp.zeros((HALF, LANES), jnp.float32)
    pair = 3 * sections
    for section in range(sections):

        def with_vis(time, carry):
            cross_real, cross_imag, power = carry
            real, imag = model_ref[0, section, time, 0], model_ref[0, section, time, 1]
            vis_real = vis_ref[0, time, pl.ds(0, HALF, 2), :]
            vis_imag = vis_ref[0, time, pl.ds(1, HALF, 2), :]
            return (
                cross_real + (vis_real * real + vis_imag * imag),
                cross_imag + (vis_imag * real - vis_real * imag),
                power + (real * real + imag * imag),
            )

        cross_real, cross_imag, power = lax.fori_loop(0, times, with_vis, (zero, zero, zero), unroll=4)
        cross_real += prior_ref[section, 0] * power
        cross_imag += prior_ref[section, 1] * power
        for other in range(section):

            def with_model(time, carry):
                pair_real, pair_imag = carry
                real, imag = model_ref[0, section, time, 0], model_ref[0, section, time, 1]
                other_real, other_imag = model_ref[0, other, time, 0], model_ref[0, other, time, 1]
                return (
                    pair_real + (other_real * real + other_imag * imag),
                    pair_imag + (other_imag * real - other_real * imag),
                )

            pair_real, pair_imag = lax.fori_loop(0, times, with_model, (zero, zero), unroll=4)
            prior_real, prior_imag = prior_ref[other, 0], prior_ref[other, 1]
            cross_real += prior_real * pair_real - prior_imag * pair_imag
            cross_imag += prior_real * pair_imag + prior_imag * pair_real
            sums_ref[0, pl.ds(head_rows + pair * HALF, HALF), :] = pair_real
            sums_ref[0, pl.ds(head_rows + (pair + 1) * HALF, HALF), :] = pair_imag
            pair += 2
        sums_ref[0, pl.ds(head_rows + 3 * section * HALF, HALF), :] = cross_real
        sums_ref[0, pl.ds(head_rows + (3 * section + 1) * HALF, HALF), :] = cross_imag
        sums_ref[0, pl.ds(head_rows + (3 * section + 2) * HALF, HALF), :] = power


def each(count, body):
    if count <= 4:
        for index in range(count):
            body(index)
    else:
        lax.fori_loop(0, count, lambda index, carry: (body(index), carry)[1], 0)


def solve_kernel(
    sections,
    intervals,
    tiles,
    dirs,
    pols,
    sums_ref,
    out_ref,
    part_ref,
    tile_ref,
    gain_msg_ref,
    square_ref,
    turned_ref,
    gain_ref,
    normal_ref,
    final_ref,
    own_sem,
    part_send,
    part_recv,
    tile_send,
    tile_recv,
    gain_send,
    gain_recv,
):
    group = dirs * pols
    rows = sums_ref.shape[1]
    head = 8 + 3 * HALF
    pieces = ((0, head), (head, rows - head)) if rows > head else ((0, rows),)
    here = lax.axis_index("bl")
    me = lax.axis_index("dir") * pols + lax.axis_index("pol")

    def group_peer(step):
        peer = lax.rem(me + step, group)
        return peer, {"dir": peer // pols, "pol": lax.rem(peer, pols)}

    own = pltpu.make_async_copy(
        sums_ref.at[lax.rem(me, intervals)], part_ref.at[group - 1], own_sem
    )
    own.start()
    barrier = pltpu.get_barrier_semaphore()
    for step in range(1, group):
        pl.semaphore_signal(barrier, inc=1, device_id=group_peer(step)[1], device_id_type=MESH)
    for step in range(1, tiles):
        pl.semaphore_signal(
            barrier, inc=1, device_id={"bl": lax.rem(here + step, tiles)}, device_id_type=MESH
        )
    pl.semaphore_wait(barrier, group - 1 + tiles - 1)

    part_copies, tile_copies = [], []
    for piece, (start, size) in enumerate(pieces):
        for step in range(1, group):
            peer, where = group_peer(step)
            part_copies.append(
                pltpu.make_async_remote_copy(
                    src_ref=sums_ref.at[lax.rem(peer, intervals), pl.ds(start, size), :],
                    dst_ref=part_ref.at[step - 1, pl.ds(start, size), :],
                    send_sem=part_send.at[piece, step - 1],
                    recv_sem=part_recv.at[piece, step - 1],
                    device_id=where,
                    device_id_type=MESH,
                )
            )
            part_copies[-1].start()
    own.wait()
    for piece, (start, size) in enumerate(pieces):
        for step in range(1, group):
            part_copies[piece * (group - 1) + step - 1].wait_recv()
        span = pl.ds(start, size)
        total = part_ref[group - 1, span, :]
        for step in range(1, group):
            total += part_ref[step - 1, span, :]
        tile_ref[here, span, :] = total
        for step in range(1, tiles):
            tile_copies.append(
                pltpu.make_async_remote_copy(
                    src_ref=tile_ref.at[here, span, :],
                    dst_ref=tile_ref.at[here, span, :],
                    send_sem=tile_send.at[piece, step - 1],
                    recv_sem=tile_recv.at[piece, step - 1],
                    device_id={"bl": lax.rem(here + step, tiles)},
                    device_id_type=MESH,
                )
            )
            tile_copies[-1].start()
    for step in range(1, tiles):
        tile_copies[step - 1].wait_recv()

    sides = 2 * tiles
    ids = jnp.concatenate(
        [tile_ref[k, 0:1, :] for k in range(tiles)] + [tile_ref[k, 1:2, :] for k in range(tiles)],
        axis=0,
    )

    def shared_sum(values):
        total = jnp.zeros((sides, LANES), jnp.float32)
        for side in range(sides):
            total += jnp.where(ids == ids[side : side + 1], values[side : side + 1], 0.0)
        return total

    def unpack(tile, slot, index):
        packed = tile_ref[tile, pl.ds(8 + index * HALF, HALF), :]
        square_ref[tile, slot, pl.ds(0, HALF, 2), :] = packed
        square_ref[tile, slot, pl.ds(1, HALF, 2), :] = swap_halves(packed)

    def normals_of(real, imag, power, gain_real, gain_imag, sign):
        square = gain_real * gain_real + gain_imag * gain_imag
        if sign > 0:
            first, second = real * gain_real - imag * gain_imag, real * gain_imag + imag * gain_real
        else:
            first, second = real * gain_real + imag * gain_imag, real * gain_imag - imag * gain_real
        return [
            jnp.sum(values, axis=0, keepdims=True) for values in (first, second, power * square)
        ]

    pair = 3 * sections
    for section in range(sections):
        if section == 1:
            for step in range(1, tiles):
                tile_copies[tiles - 1 + step - 1].wait_recv()

        def load_tile(tile, section=section, pair=pair):
            for slot in range(3):
                unpack(tile, slot, 3 * section + slot)
            for other in range(section):
                unpack(tile, 3, pair + 2 * other)
                unpack(tile, 4, pair + 2 * other + 1)
                left_real, left_imag = columns(
                    [final_ref[other, 0, pl.ds(tile, 1), :], final_ref[other, 1, pl.ds(tile, 1), :]]
                )
                right_real = final_ref[other, 0, pl.ds(tiles + tile, 1), :]
                right_imag = final_ref[other, 1, pl.ds(tiles + tile, 1), :]
                outer_real = left_real * right_real + left_imag * right_imag
                outer_imag = left_imag * right_real - left_real * right_imag
                pair_real, pair_imag = square_ref[tile, 3], square_ref[tile, 4]
                square_ref[tile, 0] -= outer_real * pair_real - outer_imag * pair_imag
                square_ref[tile, 1] -= outer_real * pair_imag + outer_imag * pair_real
            for slot in range(3):
                turned = square_ref[tile, slot].T[:ABLK, :]
                turned_ref[tile, slot, :, pl.ds(0, ABLK)] = turned

        each(tiles, load_tile)
        pair += 2 * section

        gain_ref[0] = jnp.ones((sides, LANES), jnp.float32)
        gain_ref[1] = jnp.zeros((sides, LANES), jnp.float32)
        for _ in range(ITERS):

            def tile_normals(tile):
                left_real, left_imag, right_real, right_imag = columns(
                    [
                        gain_ref[0, pl.ds(tile, 1), :],
                        gain_ref[1, pl.ds(tile, 1), :],
                        gain_ref[0, pl.ds(tiles + tile, 1), :],
                        gain_ref[1, pl.ds(tiles + tile, 1), :],
                    ]
                )
                for slot, values in enumerate(
                    normals_of(
                        turned_ref[tile, 0],
                        turned_ref[tile, 1],
                        turned_ref[tile, 2],
                        right_real,
                        right_imag,
                        1,
                    )
                ):
                    normal_ref[slot, pl.ds(tile, 1), :] = values
                for slot, values in enumerate(
                    normals_of(
                        square_ref[tile, 0],
                        square_ref[tile, 1],
                        square_ref[tile, 2],
                        left_real,
                        left_imag,
                        -1,
                    )
                ):
                    normal_ref[slot, pl.ds(tiles + tile, 1), :] = values

            each(tiles, tile_normals)
            gain_real, gain_imag = gain_ref[0], gain_ref[1]
            below = shared_sum(normal_ref[2]) + LAMBDA
            gain_ref[0] = 0.5 * (
                gain_real + (shared_sum(normal_ref[0]) + LAMBDA * gain_real) / below
            )
            gain_ref[1] = 0.5 * (
                gain_imag + (shared_sum(normal_ref[1]) + LAMBDA * gain_imag) / below
            )
        final_ref[section] = gain_ref[...]

    for section in range(sections):
        gain_msg_ref[me, section] = jnp.concatenate(
            [
                final_ref[section, kind, pl.ds(side, 1), :]
                for side in (here, tiles + here)
                for kind in (0, 1)
            ]
            + [jnp.zeros((4, LANES), jnp.float32)],
            axis=0,
        )
    copies = []
    for step in range(1, group):
        copies.append(
            pltpu.make_async_remote_copy(
                src_ref=gain_msg_ref.at[me],
                dst_ref=gain_msg_ref.at[me],
                send_sem=gain_send.at[step - 1],
                recv_sem=gain_recv.at[step - 1],
                device_id=group_peer(step)[1],
                device_id_type=MESH,
            )
        )
        copies[-1].start()
    for copy in part_copies + tile_copies:
        copy.wait_send()
    for copy in copies:
        copy.wait()
    for interval in range(intervals):
        out_ref[interval] = gain_msg_ref[interval]


def residual_kernel(
    sections, times, dir_ref, vis_ref, model_ref, prior_ref, gain_ref, out_ref, factor_ref, column_ref
):
    for section in range(sections):
        rows = [gain_ref[0, section, k : k + 1, :] for k in range(4)]
        real, imag = outer_packed(
            rows[0], rows[1], both_halves(rows[2]), both_halves(rows[3]), column_ref
        )
        factor_ref[section, 0] = prior_ref[section, 0] - real
        factor_ref[section, 1] = prior_ref[section, 1] - imag

    def sample(time, carry):
        real = vis_ref[0, time, pl.ds(0, HALF, 2), :]
        imag = vis_ref[0, time, pl.ds(1, HALF, 2), :]
        for section in range(sections):
            model_real = model_ref[0, section, time, 0]
            model_imag = model_ref[0, section, time, 1]
            factor_real, factor_imag = factor_ref[section, 0], factor_ref[section, 1]
            real += factor_real * model_real - factor_imag * model_imag
            imag += factor_real * model_imag + factor_imag * model_real
        out_ref[0, time, pl.ds(0, HALF, 2), :] = real
        out_ref[0, time, pl.ds(1, HALF, 2), :] = imag
        return carry

    lax.fori_loop(0, times, sample, 0, unroll=4)


def on_device(
    visibilities,
    hour_angle,
    antenna_layout_coords,
    point_coords,
    point_flux,
    counts,
    peel_order,
    earlier_gain_amplitude,
    earlier_gain_phase,
    tile_blocks,
):
    sections, dirs = point_coords.shape[0], lax.axis_size("dir")
    pols, tiles = lax.axis_size("pol"), lax.axis_size("bl")
    group = dirs * pols
    comps = point_flux.shape[1]
    intervals, total_times = visibilities.shape[0], visibilities.shape[3]
    times = total_times // dirs
    me_dir = lax.axis_index("dir")
    assert group % intervals == 0 and group >= intervals

    vis = visibilities.reshape(intervals, total_times, 2, HALF, LANES)
    vis = vis.transpose(0, 1, 3, 2, 4).reshape(intervals, total_times, ABLK, LANES)
    place = me_dir[None].astype(jnp.int32)

    count = 3 * sections + sections * (sections - 1)
    rows = 8 + count * HALF
    whole = lambda shape: pl.BlockSpec(shape, lambda i, *s: (0,) * len(shape))
    vis_spec = pl.BlockSpec((1, times, ABLK, LANES), lambda i, *s: (i, s[0][0], 0, 0))
    model_spec = pl.BlockSpec(
        (1, sections, times, 2, HALF, LANES), lambda i, *s: (i, 0, 0, 0, 0, 0)
    )
    prior_shape = (sections, 2, HALF, LANES)
    limit = 48 * 1024 * 1024
    model, sums, prior = pl.pallas_call(
        functools.partial(model_kernel, sections, times, comps, 2),
        out_shape=(
            jax.ShapeDtypeStruct((intervals, sections, times, 2, HALF, LANES), jnp.float32),
            jax.ShapeDtypeStruct((intervals, rows, LANES), jnp.float32),
            jax.ShapeDtypeStruct(prior_shape, jnp.float32),
        ),
        grid_spec=pltpu.PrefetchScalarGridSpec(
            num_scalar_prefetch=4,
            grid=(intervals,),
            in_specs=[
                whole(antenna_layout_coords.shape),
                whole(point_coords.shape),
                whole(point_flux.shape),
                whole(earlier_gain_amplitude.shape),
                whole(earlier_gain_phase.shape),
                pl.BlockSpec((1, 1, total_times), lambda i, *s: (i, 0, 0)),
                vis_spec,
            ],
            out_specs=(
                model_spec,
                pl.BlockSpec((1, rows, LANES), lambda i, *s: (i, 0, 0)),
                whole(prior_shape),
            ),
            scratch_shapes=[
                pltpu.VMEM((4, ABLK, CHUNK), jnp.float32),
                pltpu.VMEM((sections, 1, comps), jnp.float32),
                pltpu.VMEM((2, ABLK, LANES), jnp.float32),
                pltpu.VMEM((sections, times, comps), jnp.float32),
                pltpu.VMEM((sections, times, comps), jnp.float32),
            ],
        ),
        compiler_params=pltpu.CompilerParams(vmem_limit_bytes=limit),
        name="models",
    )(
        place,
        peel_order,
        counts,
        tile_blocks,
        antenna_layout_coords,
        point_coords,
        point_flux,
        earlier_gain_amplitude,
        earlier_gain_phase,
        hour_angle,
        vis,
    )

    dma = pltpu.SemaphoreType.DMA
    gains = pl.pallas_call(
        functools.partial(solve_kernel, sections, intervals, tiles, dirs, pols),
        out_shape=jax.ShapeDtypeStruct((intervals, sections, 8, LANES), jnp.float32),
        in_specs=[pl.BlockSpec(memory_space=pl.ANY)],
        out_specs=pl.BlockSpec(memory_space=pltpu.VMEM),
        scratch_shapes=[
            pltpu.VMEM((group, rows, LANES), jnp.float32),
            pltpu.VMEM((tiles, rows, LANES), jnp.float32),
            pltpu.VMEM((group, sections, 8, LANES), jnp.float32),
            pltpu.VMEM((tiles, 5, ABLK, LANES), jnp.float32),
            pltpu.VMEM((tiles, 3, ABLK, LANES), jnp.float32),
            pltpu.VMEM((2, 2 * tiles, LANES), jnp.float32),
            pltpu.VMEM((3, 2 * tiles, LANES), jnp.float32),
            pltpu.VMEM((sections, 2, 2 * tiles, LANES), jnp.float32),
            dma,
            dma((2, group - 1)),
            dma((2, group - 1)),
            dma((2, tiles - 1)),
            dma((2, tiles - 1)),
            dma((group - 1,)),
            dma((group - 1,)),
        ],
        compiler_params=pltpu.CompilerParams(
            collective_id=0, has_side_effects=True, vmem_limit_bytes=56 * 1024 * 1024
        ),
        name="solve",
    )(sums)

    out = pl.pallas_call(
        functools.partial(residual_kernel, sections, times),
        out_shape=jax.ShapeDtypeStruct((intervals, times, ABLK, LANES), jnp.float32),
        grid_spec=pltpu.PrefetchScalarGridSpec(
            num_scalar_prefetch=1,
            grid=(intervals,),
            in_specs=[
                vis_spec,
                model_spec,
                whole(prior_shape),
                pl.BlockSpec((1, sections, 8, LANES), lambda i, *s: (i, 0, 0, 0)),
            ],
            out_specs=pl.BlockSpec((1, times, ABLK, LANES), lambda i, *s: (i, 0, 0, 0)),
            scratch_shapes=[
                pltpu.VMEM((sections, 2, HALF, LANES), jnp.float32),
                pltpu.VMEM((2, ABLK, LANES), jnp.float32),
            ],
        ),
        compiler_params=pltpu.CompilerParams(vmem_limit_bytes=limit),
        name="residual",
    )(place, vis, model, prior, gains)
    out = out.reshape(intervals, times, HALF, 2, LANES).transpose(0, 1, 3, 2, 4)
    return out.reshape(intervals, 1, 1, times, 2, HALF * LANES)


def solution(mesh):
    placed = (
        P("band", "bl", "pol", None, None, None),
        P(None, "pol", None),
        P(),
        P(),
        P(),
        P(),
        P(),
        P("band", None),
        P("band", None),
        P("bl", None),
    )
    return jax.shard_map(
        on_device,
        mesh=mesh,
        in_specs=placed,
        out_specs=P("band", "bl", "pol", "dir", None, None),
        check_vma=False,
    )
```

```python
import functools

import jax
import jax.numpy as jnp
from jax import lax
from jax.experimental import pallas as pl
from jax.experimental.pallas import tpu as pltpu
from jax.sharding import PartitionSpec as P

ABLK = 64
ITERS = 3
LAMBDA = 1.0
HALF = ABLK // 2
LANES = 2 * ABLK
CHUNK = 128
MESH = pl.DeviceIdType.MESH
SIN_C = (4.442867911308811, -7.307443741853454, 3.5947910749268956, -0.784381842458349)
COS_C = (1.4142040873683897, -6.977642700991201, 5.715246760161864, -1.7283748369726175)


def half_turns(turns):
    part = turns - jnp.round(turns)
    square = part * part
    sine = SIN_C[-1]
    for value in SIN_C[-2::-1]:
        sine = sine * square + value
    cosine = COS_C[-1]
    for value in COS_C[-2::-1]:
        cosine = cosine * square + value
    return part * sine, cosine


def swap_halves(values):
    return pltpu.roll(values, ABLK, 1)


def predict_sample(chunks, pos_ref, east_row, north_row, weight_row):
    left_cos, left_sin, right_cos, right_sin = [], [], [], []
    for chunk in range(chunks):
        lanes = slice(chunk * CHUNK, (chunk + 1) * CHUNK)
        east, north, weight = east_row[:, lanes], north_row[:, lanes], weight_row[:, lanes]
        sine, cosine = half_turns(pos_ref[0] * east + pos_ref[1] * north)
        left_cos.append((1.0 - sine * sine).astype(jnp.bfloat16))
        left_sin.append((sine * cosine).astype(jnp.bfloat16))
        sine, cosine = half_turns(pos_ref[2] * east + pos_ref[3] * north)
        weighted = sine * weight
        right_cos.append((weight - weighted * sine).astype(jnp.bfloat16))
        right_sin.append((weighted * cosine).astype(jnp.bfloat16))
    left = jnp.concatenate(
        [jnp.concatenate(left_cos, axis=1), jnp.concatenate(left_sin, axis=1)], axis=0
    )
    right = jnp.concatenate(
        [jnp.concatenate(right_cos, axis=1), jnp.concatenate(right_sin, axis=1)], axis=0
    )
    out = lax.dot_general(
        left, right, (((1,), (1,)), ((), ())), preferred_element_type=jnp.float32
    )
    cos_even, cos_odd = out[:HALF], out[HALF:ABLK]
    sin_even, sin_odd = out[ABLK : ABLK + HALF], out[ABLK + HALF :]
    first = lax.broadcasted_iota(jnp.int32, (HALF, LANES), 1) < ABLK
    real = jnp.where(first, cos_even, swap_halves(cos_odd)) + jnp.where(
        first, swap_halves(sin_even), sin_odd
    )
    imag = jnp.where(first, sin_even, swap_halves(sin_odd)) - jnp.where(
        first, swap_halves(cos_even), cos_odd
    )
    return real, imag


def columns(rows):
    count = len(rows)
    pad = jnp.zeros((8 - count, LANES), jnp.float32)
    turned = jnp.concatenate(list(rows) + [pad], axis=0).T
    return [jnp.broadcast_to(turned[:ABLK, k : k + 1], (ABLK, LANES)) for k in range(count)]


def both_halves(row):
    first = lax.broadcasted_iota(jnp.int32, (1, LANES), 1) < ABLK
    return jnp.where(first, row, swap_halves(row))


def outer_packed(left_real, left_imag, right_real, right_imag, column_ref):
    first = lax.broadcasted_iota(jnp.int32, (HALF, LANES), 1) < ABLK
    packed = []
    for slot, column in enumerate(columns([left_real, left_imag])):
        column_ref[slot] = column
        packed.append(
            jnp.where(
                first,
                column_ref[slot, pl.ds(0, HALF, 2), :],
                column_ref[slot, pl.ds(1, HALF, 2), :],
            )
        )
    real, imag = packed
    return real * right_real + imag * right_imag, imag * right_real - real * right_imag


def pick_row(values, row):
    here = lax.broadcasted_iota(jnp.int32, values.shape, 0) == row
    return jnp.sum(jnp.where(here, values, 0.0), axis=0, keepdims=True)


def block_row(ref, row, block):
    start = pl.multiple_of((block // 2) * LANES, LANES)
    both = pick_row(ref[:, pl.ds(start, LANES)], row)
    return jnp.where(lax.rem(block, 2) == 1, swap_halves(both), both)


def model_kernel(
    sections,
    times,
    comps,
    unroll,
    dir_ref,
    order_ref,
    counts_ref,
    blocks_ref,
    layout_ref,
    coords_ref,
    flux_ref,
    amplitude_ref,
    angle_ref,
    hour_ref,
    vis_ref,
    model_ref,
    sums_ref,
    prior_ref,
    pos_ref,
    weight_ref,
    column_ref,
    east_ref,
    north_ref,
):
    left_block, right_block = blocks_ref[0, 0], blocks_ref[0, 1]

    @pl.when(pl.program_id(0) == 0)
    def _():
        sides = columns(
            [
                block_row(layout_ref, 0, left_block),
                block_row(layout_ref, 1, left_block),
                block_row(layout_ref, 0, right_block),
                block_row(layout_ref, 1, right_block),
            ]
        )
        for slot in range(2):
            column_ref[slot] = sides[slot]
            pos_ref[slot, pl.ds(0, HALF), :] = column_ref[slot, pl.ds(0, HALF, 2), :]
            pos_ref[slot, pl.ds(HALF, HALF), :] = column_ref[slot, pl.ds(1, HALF, 2), :]
            pos_ref[2 + slot] = sides[2 + slot]
        for section in range(sections):
            direction = order_ref[section]
            live = lax.broadcasted_iota(jnp.int32, (1, comps), 1) < counts_ref[direction]
            weight_ref[section] = jnp.where(live, pick_row(flux_ref[...], direction), 0.0)
            rows = []
            for block in (left_block, right_block):
                amplitude = block_row(amplitude_ref, direction, block)
                angle = block_row(angle_ref, direction, block)
                rows += [amplitude * jnp.cos(angle), amplitude * jnp.sin(angle)]
            real, imag = outer_packed(
                rows[0], rows[1], both_halves(rows[2]), both_halves(rows[3]), column_ref
            )
            prior_ref[section, 0] = real
            prior_ref[section, 1] = imag

    hour_row = hour_ref[0]
    hour_row = jnp.concatenate(
        [hour_row, jnp.zeros((1, LANES - hour_row.shape[1]), jnp.float32)], axis=1
    )
    turned = jnp.concatenate(
        [jnp.cos(hour_row), jnp.sin(hour_row), jnp.zeros((6, LANES), jnp.float32)], axis=0
    ).T
    column_ref[0] = jnp.broadcast_to(turned[:ABLK, 0:1], (ABLK, LANES))
    column_ref[1] = jnp.broadcast_to(turned[:ABLK, 1:2], (ABLK, LANES))
    start = dir_ref[0] * times
    hour_cos = column_ref[0, pl.ds(start, times), :]
    hour_sin = column_ref[1, pl.ds(start, times), :]
    for section in range(sections):
        direction = order_ref[section]
        l_row, m_row = coords_ref[direction, 0:1, :], coords_ref[direction, 1:2, :]
        for chunk in range(comps // CHUNK):
            lanes = pl.ds(chunk * CHUNK, CHUNK)
            l_part = l_row[:, chunk * CHUNK : (chunk + 1) * CHUNK]
            m_part = m_row[:, chunk * CHUNK : (chunk + 1) * CHUNK]
            east_ref[section, :, lanes] = l_part * hour_cos + m_part * hour_sin
            north_ref[section, :, lanes] = m_part * hour_cos - l_part * hour_sin

    head_rows = 8
    side = lax.broadcasted_iota(jnp.int32, (head_rows, LANES), 0)
    sums_ref[0, pl.ds(0, head_rows), :] = jnp.where(
        side == 0, left_block, jnp.where(side == 1, right_block, 0)
    ).astype(jnp.float32)

    def one_section(section):
        weight_row = weight_ref[section]

        def run(chunks):
            def sample(time, carry):
                real, imag = predict_sample(
                    chunks,
                    pos_ref,
                    east_ref[section, pl.ds(time, 1), :],
                    north_ref[section, pl.ds(time, 1), :],
                    weight_row,
                )
                model_ref[0, section, time, 0] = real
                model_ref[0, section, time, 1] = imag
                return carry

            lax.fori_loop(0, times, sample, 0, unroll=unroll)

        most = comps // CHUNK
        needed = jnp.clip((counts_ref[order_ref[section]] + CHUNK - 1) // CHUNK, 1, most)
        for chunks in range(1, most + 1):
            pl.when(needed == chunks)(functools.partial(run, chunks))

    if sections <= 2:
        for section in range(sections):
            one_section(section)
    else:
        lax.fori_loop(0, sections, lambda s, c: (one_section(s), c)[1], 0)

    zero = jnp.zeros((HALF, LANES), jnp.float32)
    pair = 3 * sections
    for section in range(sections):

        def with_vis(time, carry):
            cross_real, cross_imag, power = carry
            real, imag = model_ref[0, section, time, 0], model_ref[0, section, time, 1]
            vis_real = vis_ref[0, time, pl.ds(0, HALF, 2), :]
            vis_imag = vis_ref[0, time, pl.ds(1, HALF, 2), :]
            return (
                cross_real + (vis_real * real + vis_imag * imag),
                cross_imag + (vis_imag * real - vis_real * imag),
                power + (real * real + imag * imag),
            )

        cross_real, cross_imag, power = lax.fori_loop(0, times, with_vis, (zero, zero, zero), unroll=4)
        cross_real += prior_ref[section, 0] * power
        cross_imag += prior_ref[section, 1] * power
        for other in range(section):

            def with_model(time, carry):
                pair_real, pair_imag = carry
                real, imag = model_ref[0, section, time, 0], model_ref[0, section, time, 1]
                other_real, other_imag = model_ref[0, other, time, 0], model_ref[0, other, time, 1]
                return (
                    pair_real + (other_real * real + other_imag * imag),
                    pair_imag + (other_imag * real - other_real * imag),
                )

            pair_real, pair_imag = lax.fori_loop(0, times, with_model, (zero, zero), unroll=4)
            prior_real, prior_imag = prior_ref[other, 0], prior_ref[other, 1]
            cross_real += prior_real * pair_real - prior_imag * pair_imag
            cross_imag += prior_real * pair_imag + prior_imag * pair_real
            sums_ref[0, pl.ds(head_rows + pair * HALF, HALF), :] = pair_real
            sums_ref[0, pl.ds(head_rows + (pair + 1) * HALF, HALF), :] = pair_imag
            pair += 2
        sums_ref[0, pl.ds(head_rows + 3 * section * HALF, HALF), :] = cross_real
        sums_ref[0, pl.ds(head_rows + (3 * section + 1) * HALF, HALF), :] = cross_imag
        sums_ref[0, pl.ds(head_rows + (3 * section + 2) * HALF, HALF), :] = power


def each(count, body):
    if count <= 4:
        for index in range(count):
            body(index)
    else:
        lax.fori_loop(0, count, lambda index, carry: (body(index), carry)[1], 0)


def solve_kernel(
    sections,
    intervals,
    tiles,
    dirs,
    pols,
    sums_ref,
    out_ref,
    part_ref,
    tile_ref,
    gain_msg_ref,
    square_ref,
    turned_ref,
    gain_ref,
    normal_ref,
    final_ref,
    own_sem,
    part_send,
    part_recv,
    tile_send,
    tile_recv,
    gain_send,
    gain_recv,
):
    group = dirs * pols
    rows = sums_ref.shape[1]
    head = 8 + 3 * HALF
    pieces = ((0, head), (head, rows - head)) if rows > head else ((0, rows),)
    here = lax.axis_index("bl")
    me = lax.axis_index("dir") * pols + lax.axis_index("pol")

    def group_peer(step):
        peer = lax.rem(me + step, group)
        return peer, {"dir": peer // pols, "pol": lax.rem(peer, pols)}

    own = pltpu.make_async_copy(
        sums_ref.at[lax.rem(me, intervals)], part_ref.at[group - 1], own_sem
    )
    own.start()
    barrier = pltpu.get_barrier_semaphore()
    for step in range(1, group):
        pl.semaphore_signal(barrier, inc=1, device_id=group_peer(step)[1], device_id_type=MESH)
    for step in range(1, tiles):
        pl.semaphore_signal(
            barrier, inc=1, device_id={"bl": lax.rem(here + step, tiles)}, device_id_type=MESH
        )
    pl.semaphore_wait(barrier, group - 1 + tiles - 1)

    part_copies, tile_copies = [], []
    for piece, (start, size) in enumerate(pieces):
        for step in range(1, group):
            peer, where = group_peer(step)
            part_copies.append(
                pltpu.make_async_remote_copy(
                    src_ref=sums_ref.at[lax.rem(peer, intervals), pl.ds(start, size), :],
                    dst_ref=part_ref.at[step - 1, pl.ds(start, size), :],
                    send_sem=part_send.at[piece, step - 1],
                    recv_sem=part_recv.at[piece, step - 1],
                    device_id=where,
                    device_id_type=MESH,
                )
            )
            part_copies[-1].start()
    own.wait()
    for piece, (start, size) in enumerate(pieces):
        for step in range(1, group):
            part_copies[piece * (group - 1) + step - 1].wait_recv()
        span = pl.ds(start, size)
        total = part_ref[group - 1, span, :]
        for step in range(1, group):
            total += part_ref[step - 1, span, :]
        tile_ref[here, span, :] = total
        for step in range(1, tiles):
            tile_copies.append(
                pltpu.make_async_remote_copy(
                    src_ref=tile_ref.at[here, span, :],
                    dst_ref=tile_ref.at[here, span, :],
                    send_sem=tile_send.at[piece, step - 1],
                    recv_sem=tile_recv.at[piece, step - 1],
                    device_id={"bl": lax.rem(here + step, tiles)},
                    device_id_type=MESH,
                )
            )
            tile_copies[-1].start()
    for step in range(1, tiles):
        tile_copies[step - 1].wait_recv()

    sides = 2 * tiles
    ids = jnp.concatenate(
        [tile_ref[k, 0:1, :] for k in range(tiles)] + [tile_ref[k, 1:2, :] for k in range(tiles)],
        axis=0,
    )

    def shared_sum(values):
        total = jnp.zeros((sides, LANES), jnp.float32)
        for side in range(sides):
            total += jnp.where(ids == ids[side : side + 1], values[side : side + 1], 0.0)
        return total

    def unpack(tile, slot, index):
        packed = tile_ref[tile, pl.ds(8 + index * HALF, HALF), :]
        square_ref[tile, slot, pl.ds(0, HALF, 2), :] = packed
        square_ref[tile, slot, pl.ds(1, HALF, 2), :] = swap_halves(packed)

    def normals_of(real, imag, power, gain_real, gain_imag, sign):
        square = gain_real * gain_real + gain_imag * gain_imag
        if sign > 0:
            first, second = real * gain_real - imag * gain_imag, real * gain_imag + imag * gain_real
        else:
            first, second = real * gain_real + imag * gain_imag, real * gain_imag - imag * gain_real
        return [
            jnp.sum(values, axis=0, keepdims=True) for values in (first, second, power * square)
        ]

    pair = 3 * sections
    for section in range(sections):
        if section == 1:
            for step in range(1, tiles):
                tile_copies[tiles - 1 + step - 1].wait_recv()

        def load_tile(tile, section=section, pair=pair):
            for slot in range(3):
                unpack(tile, slot, 3 * section + slot)
            for other in range(section):
                unpack(tile, 3, pair + 2 * other)
                unpack(tile, 4, pair + 2 * other + 1)
                left_real, left_imag = columns(
                    [final_ref[other, 0, pl.ds(tile, 1), :], final_ref[other, 1, pl.ds(tile, 1), :]]
                )
                right_real = final_ref[other, 0, pl.ds(tiles + tile, 1), :]
                right_imag = final_ref[other, 1, pl.ds(tiles + tile, 1), :]
                outer_real = left_real * right_real + left_imag * right_imag
                outer_imag = left_imag * right_real - left_real * right_imag
                pair_real, pair_imag = square_ref[tile, 3], square_ref[tile, 4]
                square_ref[tile, 0] -= outer_real * pair_real - outer_imag * pair_imag
                square_ref[tile, 1] -= outer_real * pair_imag + outer_imag * pair_real
            for slot in range(3):
                turned = square_ref[tile, slot].T[:ABLK, :]
                turned_ref[tile, slot, :, pl.ds(0, ABLK)] = turned

        each(tiles, load_tile)
        pair += 2 * section

        gain_ref[0] = jnp.ones((sides, LANES), jnp.float32)
        gain_ref[1] = jnp.zeros((sides, LANES), jnp.float32)
        for _ in range(ITERS):

            def tile_normals(tile):
                left_real, left_imag, right_real, right_imag = columns(
                    [
                        gain_ref[0, pl.ds(tile, 1), :],
                        gain_ref[1, pl.ds(tile, 1), :],
                        gain_ref[0, pl.ds(tiles + tile, 1), :],
                        gain_ref[1, pl.ds(tiles + tile, 1), :],
                    ]
                )
                for slot, values in enumerate(
                    normals_of(
                        turned_ref[tile, 0],
                        turned_ref[tile, 1],
                        turned_ref[tile, 2],
                        right_real,
                        right_imag,
                        1,
                    )
                ):
                    normal_ref[slot, pl.ds(tile, 1), :] = values
                for slot, values in enumerate(
                    normals_of(
                        square_ref[tile, 0],
                        square_ref[tile, 1],
                        square_ref[tile, 2],
                        left_real,
                        left_imag,
                        -1,
                    )
                ):
                    normal_ref[slot, pl.ds(tiles + tile, 1), :] = values

            each(tiles, tile_normals)
            gain_real, gain_imag = gain_ref[0], gain_ref[1]
            below = shared_sum(normal_ref[2]) + LAMBDA
            gain_ref[0] = 0.5 * (
                gain_real + (shared_sum(normal_ref[0]) + LAMBDA * gain_real) / below
            )
            gain_ref[1] = 0.5 * (
                gain_imag + (shared_sum(normal_ref[1]) + LAMBDA * gain_imag) / below
            )
        final_ref[section] = gain_ref[...]

    for section in range(sections):
        gain_msg_ref[me, section] = jnp.concatenate(
            [
                final_ref[section, kind, pl.ds(side, 1), :]
                for side in (here, tiles + here)
                for kind in (0, 1)
            ]
            + [jnp.zeros((4, LANES), jnp.float32)],
            axis=0,
        )
    copies = []
    for step in range(1, group):
        copies.append(
            pltpu.make_async_remote_copy(
                src_ref=gain_msg_ref.at[me],
                dst_ref=gain_msg_ref.at[me],
                send_sem=gain_send.at[step - 1],
                recv_sem=gain_recv.at[step - 1],
                device_id=group_peer(step)[1],
                device_id_type=MESH,
            )
        )
        copies[-1].start()
    for copy in part_copies + tile_copies:
        copy.wait_send()
    for copy in copies:
        copy.wait()
    for interval in range(intervals):
        out_ref[interval] = gain_msg_ref[interval]


def residual_kernel(
    sections, times, dir_ref, vis_ref, model_ref, prior_ref, gain_ref, out_ref, factor_ref, column_ref
):
    for section in range(sections):
        rows = [gain_ref[0, section, k : k + 1, :] for k in range(4)]
        real, imag = outer_packed(
            rows[0], rows[1], both_halves(rows[2]), both_halves(rows[3]), column_ref
        )
        factor_ref[section, 0] = prior_ref[section, 0] - real
        factor_ref[section, 1] = prior_ref[section, 1] - imag

    def sample(time, carry):
        real = vis_ref[0, time, pl.ds(0, HALF, 2), :]
        imag = vis_ref[0, time, pl.ds(1, HALF, 2), :]
        for section in range(sections):
            model_real = model_ref[0, section, time, 0]
            model_imag = model_ref[0, section, time, 1]
            factor_real, factor_imag = factor_ref[section, 0], factor_ref[section, 1]
            real += factor_real * model_real - factor_imag * model_imag
            imag += factor_real * model_imag + factor_imag * model_real
        out_ref[0, time, pl.ds(0, HALF, 2), :] = real
        out_ref[0, time, pl.ds(1, HALF, 2), :] = imag
        return carry

    lax.fori_loop(0, times, sample, 0, unroll=4)


def on_device(
    visibilities,
    hour_angle,
    antenna_layout_coords,
    point_coords,
    point_flux,
    counts,
    peel_order,
    earlier_gain_amplitude,
    earlier_gain_phase,
    tile_blocks,
):
    sections, dirs = point_coords.shape[0], lax.axis_size("dir")
    pols, tiles = lax.axis_size("pol"), lax.axis_size("bl")
    group = dirs * pols
    comps = point_flux.shape[1]
    intervals, total_times = visibilities.shape[0], visibilities.shape[3]
    times = total_times // dirs
    me_dir = lax.axis_index("dir")
    assert group % intervals == 0 and group >= intervals

    vis = visibilities.reshape(intervals, total_times, 2, HALF, LANES)
    vis = vis.transpose(0, 1, 3, 2, 4).reshape(intervals, total_times, ABLK, LANES)
    place = me_dir[None].astype(jnp.int32)

    count = 3 * sections + sections * (sections - 1)
    rows = 8 + count * HALF
    whole = lambda shape: pl.BlockSpec(shape, lambda i, *s: (0,) * len(shape))
    vis_spec = pl.BlockSpec((1, times, ABLK, LANES), lambda i, *s: (i, s[0][0], 0, 0))
    model_spec = pl.BlockSpec(
        (1, sections, times, 2, HALF, LANES), lambda i, *s: (i, 0, 0, 0, 0, 0)
    )
    prior_shape = (sections, 2, HALF, LANES)
    limit = 62 * 1024 * 1024
    model, sums, prior = pl.pallas_call(
        functools.partial(model_kernel, sections, times, comps, 8),
        out_shape=(
            jax.ShapeDtypeStruct((intervals, sections, times, 2, HALF, LANES), jnp.float32),
            jax.ShapeDtypeStruct((intervals, rows, LANES), jnp.float32),
            jax.ShapeDtypeStruct(prior_shape, jnp.float32),
        ),
        grid_spec=pltpu.PrefetchScalarGridSpec(
            num_scalar_prefetch=4,
            grid=(intervals,),
            in_specs=[
                whole(antenna_layout_coords.shape),
                whole(point_coords.shape),
                whole(point_flux.shape),
                whole(earlier_gain_amplitude.shape),
                whole(earlier_gain_phase.shape),
                pl.BlockSpec((1, 1, total_times), lambda i, *s: (i, 0, 0)),
                vis_spec,
            ],
            out_specs=(
                model_spec,
                pl.BlockSpec((1, rows, LANES), lambda i, *s: (i, 0, 0)),
                whole(prior_shape),
            ),
            scratch_shapes=[
                pltpu.VMEM((4, ABLK, CHUNK), jnp.float32),
                pltpu.VMEM((sections, 1, comps), jnp.float32),
                pltpu.VMEM((2, ABLK, LANES), jnp.float32),
                pltpu.VMEM((sections, times, comps), jnp.float32),
                pltpu.VMEM((sections, times, comps), jnp.float32),
            ],
        ),
        compiler_params=pltpu.CompilerParams(vmem_limit_bytes=limit),
        name="models",
    )(
        place,
        peel_order,
        counts,
        tile_blocks,
        antenna_layout_coords,
        point_coords,
        point_flux,
        earlier_gain_amplitude,
        earlier_gain_phase,
        hour_angle,
        vis,
    )

    dma = pltpu.SemaphoreType.DMA
    gains = pl.pallas_call(
        functools.partial(solve_kernel, sections, intervals, tiles, dirs, pols),
        out_shape=jax.ShapeDtypeStruct((intervals, sections, 8, LANES), jnp.float32),
        in_specs=[pl.BlockSpec(memory_space=pl.ANY)],
        out_specs=pl.BlockSpec(memory_space=pltpu.VMEM),
        scratch_shapes=[
            pltpu.VMEM((group, rows, LANES), jnp.float32),
            pltpu.VMEM((tiles, rows, LANES), jnp.float32),
            pltpu.VMEM((group, sections, 8, LANES), jnp.float32),
            pltpu.VMEM((tiles, 5, ABLK, LANES), jnp.float32),
            pltpu.VMEM((tiles, 3, ABLK, LANES), jnp.float32),
            pltpu.VMEM((2, 2 * tiles, LANES), jnp.float32),
            pltpu.VMEM((3, 2 * tiles, LANES), jnp.float32),
            pltpu.VMEM((sections, 2, 2 * tiles, LANES), jnp.float32),
            dma,
            dma((2, group - 1)),
            dma((2, group - 1)),
            dma((2, tiles - 1)),
            dma((2, tiles - 1)),
            dma((group - 1,)),
            dma((group - 1,)),
        ],
        compiler_params=pltpu.CompilerParams(
            collective_id=0, has_side_effects=True, vmem_limit_bytes=62 * 1024 * 1024
        ),
        name="solve",
    )(sums)

    out = pl.pallas_call(
        functools.partial(residual_kernel, sections, times),
        out_shape=jax.ShapeDtypeStruct((intervals, times, ABLK, LANES), jnp.float32),
        grid_spec=pltpu.PrefetchScalarGridSpec(
            num_scalar_prefetch=1,
            grid=(intervals,),
            in_specs=[
                vis_spec,
                model_spec,
                whole(prior_shape),
                pl.BlockSpec((1, sections, 8, LANES), lambda i, *s: (i, 0, 0, 0)),
            ],
            out_specs=pl.BlockSpec((1, times, ABLK, LANES), lambda i, *s: (i, 0, 0, 0)),
            scratch_shapes=[
                pltpu.VMEM((sections, 2, HALF, LANES), jnp.float32),
                pltpu.VMEM((2, ABLK, LANES), jnp.float32),
            ],
        ),
        compiler_params=pltpu.CompilerParams(vmem_limit_bytes=limit),
        name="residual",
    )(place, vis, model, prior, gains)
    out = out.reshape(intervals, times, HALF, 2, LANES).transpose(0, 1, 3, 2, 4)
    return out.reshape(intervals, 1, 1, times, 2, HALF * LANES)


def solution(mesh):
    placed = (
        P("band", "bl", "pol", None, None, None),
        P(None, "pol", None),
        P(),
        P(),
        P(),
        P(),
        P(),
        P("band", None),
        P("band", None),
        P("bl", None),
    )
    return jax.shard_map(
        on_device,
        mesh=mesh,
        in_specs=placed,
        out_specs=P("band", "bl", "pol", "dir", None, None),
        check_vma=False,
    )
```

```python
import functools

import jax
import jax.numpy as jnp
from jax import lax
from jax.experimental import pallas as pl
from jax.experimental.pallas import tpu as pltpu
from jax.sharding import PartitionSpec as P

ABLK = 64
ITERS = 3
LAMBDA = 1.0
HALF = ABLK // 2
LANES = 2 * ABLK
CHUNK = 128
MESH = pl.DeviceIdType.MESH
SIN_C = (4.442867911308811, -7.307443741853454, 3.5947910749268956, -0.784381842458349)
COS_C = (1.4142040873683897, -6.977642700991201, 5.715246760161864, -1.7283748369726175)


def half_turns(turns):
    part = turns - jnp.round(turns)
    square = part * part
    sine = SIN_C[-1]
    for value in SIN_C[-2::-1]:
        sine = sine * square + value
    cosine = COS_C[-1]
    for value in COS_C[-2::-1]:
        cosine = cosine * square + value
    return part * sine, cosine


def swap_halves(values):
    return pltpu.roll(values, ABLK, 1)


def predict_sample(chunks, pos_ref, east_row, north_row, weight_row):
    left_cos, left_sin, right_cos, right_sin = [], [], [], []
    for chunk in range(chunks):
        lanes = slice(chunk * CHUNK, (chunk + 1) * CHUNK)
        east, north, weight = east_row[:, lanes], north_row[:, lanes], weight_row[:, lanes]
        sine, cosine = half_turns(pos_ref[0] * east + pos_ref[1] * north)
        left_cos.append((1.0 - sine * sine).astype(jnp.bfloat16))
        left_sin.append((sine * cosine).astype(jnp.bfloat16))
        sine, cosine = half_turns(pos_ref[2] * east + pos_ref[3] * north)
        weighted = sine * weight
        right_cos.append((weight - weighted * sine).astype(jnp.bfloat16))
        right_sin.append((weighted * cosine).astype(jnp.bfloat16))
    left = jnp.concatenate(
        [jnp.concatenate(left_cos, axis=1), jnp.concatenate(left_sin, axis=1)], axis=0
    )
    right = jnp.concatenate(
        [jnp.concatenate(right_cos, axis=1), jnp.concatenate(right_sin, axis=1)], axis=0
    )
    out = lax.dot_general(
        left, right, (((1,), (1,)), ((), ())), preferred_element_type=jnp.float32
    )
    cos_even, cos_odd = out[:HALF], out[HALF:ABLK]
    sin_even, sin_odd = out[ABLK : ABLK + HALF], out[ABLK + HALF :]
    first = lax.broadcasted_iota(jnp.int32, (HALF, LANES), 1) < ABLK
    real = jnp.where(first, cos_even, swap_halves(cos_odd)) + jnp.where(
        first, swap_halves(sin_even), sin_odd
    )
    imag = jnp.where(first, sin_even, swap_halves(sin_odd)) - jnp.where(
        first, swap_halves(cos_even), cos_odd
    )
    return real, imag


def columns(rows):
    count = len(rows)
    pad = jnp.zeros((8 - count, LANES), jnp.float32)
    turned = jnp.concatenate(list(rows) + [pad], axis=0).T
    return [jnp.broadcast_to(turned[:ABLK, k : k + 1], (ABLK, LANES)) for k in range(count)]


def both_halves(row):
    first = lax.broadcasted_iota(jnp.int32, (1, LANES), 1) < ABLK
    return jnp.where(first, row, swap_halves(row))


def outer_packed(left_real, left_imag, right_real, right_imag, column_ref):
    first = lax.broadcasted_iota(jnp.int32, (HALF, LANES), 1) < ABLK
    packed = []
    for slot, column in enumerate(columns([left_real, left_imag])):
        column_ref[slot] = column
        packed.append(
            jnp.where(
                first,
                column_ref[slot, pl.ds(0, HALF, 2), :],
                column_ref[slot, pl.ds(1, HALF, 2), :],
            )
        )
    real, imag = packed
    return real * right_real + imag * right_imag, imag * right_real - real * right_imag


def pick_row(values, row):
    here = lax.broadcasted_iota(jnp.int32, values.shape, 0) == row
    return jnp.sum(jnp.where(here, values, 0.0), axis=0, keepdims=True)


def block_row(ref, row, block):
    start = pl.multiple_of((block // 2) * LANES, LANES)
    both = pick_row(ref[:, pl.ds(start, LANES)], row)
    return jnp.where(lax.rem(block, 2) == 1, swap_halves(both), both)


def model_kernel(
    sections,
    times,
    comps,
    unroll,
    dir_ref,
    order_ref,
    counts_ref,
    blocks_ref,
    layout_ref,
    coords_ref,
    flux_ref,
    amplitude_ref,
    angle_ref,
    hour_ref,
    vis_ref,
    model_ref,
    sums_ref,
    prior_ref,
    pos_ref,
    weight_ref,
    column_ref,
    east_ref,
    north_ref,
):
    left_block, right_block = blocks_ref[0, 0], blocks_ref[0, 1]

    @pl.when(pl.program_id(0) == 0)
    def _():
        sides = columns(
            [
                block_row(layout_ref, 0, left_block),
                block_row(layout_ref, 1, left_block),
                block_row(layout_ref, 0, right_block),
                block_row(layout_ref, 1, right_block),
            ]
        )
        for slot in range(2):
            column_ref[slot] = sides[slot]
            pos_ref[slot, pl.ds(0, HALF), :] = column_ref[slot, pl.ds(0, HALF, 2), :]
            pos_ref[slot, pl.ds(HALF, HALF), :] = column_ref[slot, pl.ds(1, HALF, 2), :]
            pos_ref[2 + slot] = sides[2 + slot]
        for section in range(sections):
            direction = order_ref[section]
            live = lax.broadcasted_iota(jnp.int32, (1, comps), 1) < counts_ref[direction]
            weight_ref[section] = jnp.where(live, pick_row(flux_ref[...], direction), 0.0)
            rows = []
            for block in (left_block, right_block):
                amplitude = block_row(amplitude_ref, direction, block)
                angle = block_row(angle_ref, direction, block)
                rows += [amplitude * jnp.cos(angle), amplitude * jnp.sin(angle)]
            real, imag = outer_packed(
                rows[0], rows[1], both_halves(rows[2]), both_halves(rows[3]), column_ref
            )
            prior_ref[section, 0] = real
            prior_ref[section, 1] = imag

    hour_row = hour_ref[0]
    hour_row = jnp.concatenate(
        [hour_row, jnp.zeros((1, LANES - hour_row.shape[1]), jnp.float32)], axis=1
    )
    turned = jnp.concatenate(
        [jnp.cos(hour_row), jnp.sin(hour_row), jnp.zeros((6, LANES), jnp.float32)], axis=0
    ).T
    column_ref[0] = jnp.broadcast_to(turned[:ABLK, 0:1], (ABLK, LANES))
    column_ref[1] = jnp.broadcast_to(turned[:ABLK, 1:2], (ABLK, LANES))
    start = dir_ref[0] * times
    hour_cos = column_ref[0, pl.ds(start, times), :]
    hour_sin = column_ref[1, pl.ds(start, times), :]
    for section in range(sections):
        direction = order_ref[section]
        l_row, m_row = coords_ref[direction, 0:1, :], coords_ref[direction, 1:2, :]
        for chunk in range(comps // CHUNK):
            lanes = pl.ds(chunk * CHUNK, CHUNK)
            l_part = l_row[:, chunk * CHUNK : (chunk + 1) * CHUNK]
            m_part = m_row[:, chunk * CHUNK : (chunk + 1) * CHUNK]
            east_ref[section, :, lanes] = l_part * hour_cos + m_part * hour_sin
            north_ref[section, :, lanes] = m_part * hour_cos - l_part * hour_sin

    head_rows = 8
    side = lax.broadcasted_iota(jnp.int32, (head_rows, LANES), 0)
    sums_ref[0, pl.ds(0, head_rows), :] = jnp.where(
        side == 0, left_block, jnp.where(side == 1, right_block, 0)
    ).astype(jnp.float32)

    def one_section(section):
        weight_row = weight_ref[section]

        def run(chunks):
            def sample(time, carry):
                real, imag = predict_sample(
                    chunks,
                    pos_ref,
                    east_ref[section, pl.ds(time, 1), :],
                    north_ref[section, pl.ds(time, 1), :],
                    weight_row,
                )
                model_ref[0, section, time, 0] = real
                model_ref[0, section, time, 1] = imag
                return carry

            lax.fori_loop(0, times, sample, 0, unroll=unroll)

        most = comps // CHUNK
        needed = jnp.clip((counts_ref[order_ref[section]] + CHUNK - 1) // CHUNK, 1, most)
        for chunks in range(1, most + 1):
            pl.when(needed == chunks)(functools.partial(run, chunks))

    if sections <= 2:
        for section in range(sections):
            one_section(section)
    else:
        lax.fori_loop(0, sections, lambda s, c: (one_section(s), c)[1], 0)

    zero = jnp.zeros((HALF, LANES), jnp.float32)
    pair = 3 * sections
    for section in range(sections):

        def with_vis(time, carry):
            cross_real, cross_imag, power = carry
            real, imag = model_ref[0, section, time, 0], model_ref[0, section, time, 1]
            vis_real = vis_ref[0, time, pl.ds(0, HALF, 2), :]
            vis_imag = vis_ref[0, time, pl.ds(1, HALF, 2), :]
            return (
                cross_real + (vis_real * real + vis_imag * imag),
                cross_imag + (vis_imag * real - vis_real * imag),
                power + (real * real + imag * imag),
            )

        cross_real, cross_imag, power = lax.fori_loop(0, times, with_vis, (zero, zero, zero), unroll=4)
        cross_real += prior_ref[section, 0] * power
        cross_imag += prior_ref[section, 1] * power
        for other in range(section):

            def with_model(time, carry):
                pair_real, pair_imag = carry
                real, imag = model_ref[0, section, time, 0], model_ref[0, section, time, 1]
                other_real, other_imag = model_ref[0, other, time, 0], model_ref[0, other, time, 1]
                return (
                    pair_real + (other_real * real + other_imag * imag),
                    pair_imag + (other_imag * real - other_real * imag),
                )

            pair_real, pair_imag = lax.fori_loop(0, times, with_model, (zero, zero), unroll=4)
            prior_real, prior_imag = prior_ref[other, 0], prior_ref[other, 1]
            cross_real += prior_real * pair_real - prior_imag * pair_imag
            cross_imag += prior_real * pair_imag + prior_imag * pair_real
            sums_ref[0, pl.ds(head_rows + pair * HALF, HALF), :] = pair_real
            sums_ref[0, pl.ds(head_rows + (pair + 1) * HALF, HALF), :] = pair_imag
            pair += 2
        sums_ref[0, pl.ds(head_rows + 3 * section * HALF, HALF), :] = cross_real
        sums_ref[0, pl.ds(head_rows + (3 * section + 1) * HALF, HALF), :] = cross_imag
        sums_ref[0, pl.ds(head_rows + (3 * section + 2) * HALF, HALF), :] = power


def each(count, body):
    if count <= 4:
        for index in range(count):
            body(index)
    else:
        lax.fori_loop(0, count, lambda index, carry: (body(index), carry)[1], 0)


def solve_kernel(
    sections,
    intervals,
    tiles,
    dirs,
    pols,
    sums_ref,
    out_ref,
    part_ref,
    tile_ref,
    gain_msg_ref,
    gain_in_ref,
    square_ref,
    turned_ref,
    gain_ref,
    normal_ref,
    final_ref,
    own_sem,
    part_send,
    part_recv,
    tile_send,
    tile_recv,
    gain_send,
    gain_recv,
):
    group = dirs * pols
    rows = sums_ref.shape[1]
    head = 8 + 3 * HALF
    pieces = ((0, head), (head, rows - head)) if rows > head else ((0, rows),)
    here = lax.axis_index("bl")
    me = lax.axis_index("dir") * pols + lax.axis_index("pol")

    def group_peer(step):
        peer = lax.rem(me + step, group)
        return peer, {"dir": peer // pols, "pol": lax.rem(peer, pols)}

    solver = lax.rem(tiles // 2 - 1 + lax.rem(me, 2), tiles)
    mine = here * group + me

    def place(index):
        tile, member = index // group, lax.rem(index, group)
        return {"bl": tile, "dir": member // pols, "pol": lax.rem(member, pols)}

    own = pltpu.make_async_copy(
        sums_ref.at[lax.rem(me, intervals)], part_ref.at[group - 1], own_sem
    )
    own.start()
    everyone = tiles * group
    barrier = pltpu.get_barrier_semaphore()

    def greet(step, carry):
        pl.semaphore_signal(
            barrier,
            inc=1,
            device_id=place(lax.rem(mine + step, everyone)),
            device_id_type=MESH,
        )
        return carry

    lax.fori_loop(1, everyone, greet, 0)
    pl.semaphore_wait(barrier, everyone - 1)

    def tile_copy(piece, tile, where=None):
        span = pl.ds(*pieces[piece])
        return pltpu.make_async_remote_copy(
            src_ref=tile_ref.at[tile, span, :],
            dst_ref=tile_ref.at[tile, span, :],
            send_sem=tile_send.at[piece],
            recv_sem=tile_recv.at[piece, tile],
            device_id={"bl": solver if where is None else where},
            device_id_type=MESH,
        )

    def receive_tiles(piece):
        for tile in range(tiles):
            pl.when(here != tile)(lambda: tile_copy(piece, tile, lax.rem(here + 1, tiles)).wait_recv())

    part_copies = []
    for piece, (start, size) in enumerate(pieces):
        for step in range(1, group):
            peer, where = group_peer(step)
            part_copies.append(
                pltpu.make_async_remote_copy(
                    src_ref=sums_ref.at[lax.rem(peer, intervals), pl.ds(start, size), :],
                    dst_ref=part_ref.at[step - 1, pl.ds(start, size), :],
                    send_sem=part_send.at[piece, step - 1],
                    recv_sem=part_recv.at[piece, step - 1],
                    device_id=where,
                    device_id_type=MESH,
                )
            )
            part_copies[-1].start()
    own.wait()
    for piece, (start, size) in enumerate(pieces):
        for step in range(1, group):
            part_copies[piece * (group - 1) + step - 1].wait_recv()
        span = pl.ds(start, size)
        total = part_ref[group - 1, span, :]
        for step in range(1, group):
            total += part_ref[step - 1, span, :]
        tile_ref[here, span, :] = total
        pl.when(here != solver)(tile_copy(piece, here).start)

    def gain_copy(interval, target):
        return pltpu.make_async_remote_copy(
            src_ref=gain_msg_ref.at[target // group],
            dst_ref=gain_in_ref.at[interval],
            send_sem=gain_send.at[target],
            recv_sem=gain_recv.at[interval],
            device_id=place(target),
            device_id_type=MESH,
        )

    @pl.when(here == solver)
    def _():
        receive_tiles(0)
        solve_tiles(
            sections, tiles, tile_ref, square_ref, turned_ref, gain_ref, normal_ref, final_ref,
            lambda: receive_tiles(1),
        )
        for section in range(sections):

            def pack(tile, section=section):
                gain_msg_ref[tile, section] = jnp.concatenate(
                    [
                        final_ref[section, kind, pl.ds(side, 1), :]
                        for side in (tile, tiles + tile)
                        for kind in (0, 1)
                    ]
                    + [jnp.zeros((4, LANES), jnp.float32)],
                    axis=0,
                )

            each(tiles, pack)

    sends = (here == solver) & (me < intervals)

    @pl.when(sends)
    def _():
        def start(step, carry):
            gain_copy(me, lax.rem(mine + step, everyone)).start()
            return carry

        lax.fori_loop(1, everyone, start, 0)
        gain_in_ref[me] = gain_msg_ref[here]

    for copy in part_copies:
        copy.wait_send()
    for piece in range(len(pieces)):
        pl.when(here != solver)(tile_copy(piece, here).wait_send)
    for interval in range(intervals):
        pl.when(jnp.logical_not(sends & (me == interval)))(
            lambda: gain_copy(interval, lax.rem(mine + 1, everyone)).wait_recv()
        )
        out_ref[interval] = gain_in_ref[interval]

    @pl.when(sends)
    def _():
        def finish(step, carry):
            gain_copy(me, lax.rem(mine + step, everyone)).wait_send()
            return carry

        lax.fori_loop(1, everyone, finish, 0)


def solve_tiles(
    sections, tiles, tile_ref, square_ref, turned_ref, gain_ref, normal_ref, final_ref, receive_rest
):
    sides = 2 * tiles
    ids = jnp.concatenate(
        [tile_ref[k, 0:1, :] for k in range(tiles)] + [tile_ref[k, 1:2, :] for k in range(tiles)],
        axis=0,
    )

    def shared_sum(values):
        total = jnp.zeros((sides, LANES), jnp.float32)
        for side in range(sides):
            total += jnp.where(ids == ids[side : side + 1], values[side : side + 1], 0.0)
        return total

    def unpack(tile, slot, index):
        packed = tile_ref[tile, pl.ds(8 + index * HALF, HALF), :]
        square_ref[tile, slot, pl.ds(0, HALF, 2), :] = packed
        square_ref[tile, slot, pl.ds(1, HALF, 2), :] = swap_halves(packed)

    def normals_of(real, imag, power, gain_real, gain_imag, sign):
        square = gain_real * gain_real + gain_imag * gain_imag
        if sign > 0:
            first, second = real * gain_real - imag * gain_imag, real * gain_imag + imag * gain_real
        else:
            first, second = real * gain_real + imag * gain_imag, real * gain_imag - imag * gain_real
        return [
            jnp.sum(values, axis=0, keepdims=True) for values in (first, second, power * square)
        ]

    pair = 3 * sections
    for section in range(sections):
        if section == 1:
            receive_rest()

        def load_tile(tile, section=section, pair=pair):
            for slot in range(3):
                unpack(tile, slot, 3 * section + slot)
            for other in range(section):
                unpack(tile, 3, pair + 2 * other)
                unpack(tile, 4, pair + 2 * other + 1)
                left_real, left_imag = columns(
                    [final_ref[other, 0, pl.ds(tile, 1), :], final_ref[other, 1, pl.ds(tile, 1), :]]
                )
                right_real = final_ref[other, 0, pl.ds(tiles + tile, 1), :]
                right_imag = final_ref[other, 1, pl.ds(tiles + tile, 1), :]
                outer_real = left_real * right_real + left_imag * right_imag
                outer_imag = left_imag * right_real - left_real * right_imag
                pair_real, pair_imag = square_ref[tile, 3], square_ref[tile, 4]
                square_ref[tile, 0] -= outer_real * pair_real - outer_imag * pair_imag
                square_ref[tile, 1] -= outer_real * pair_imag + outer_imag * pair_real
            for slot in range(3):
                turned = square_ref[tile, slot].T[:ABLK, :]
                turned_ref[tile, slot, :, pl.ds(0, ABLK)] = turned

        each(tiles, load_tile)
        pair += 2 * section

        gain_ref[0] = jnp.ones((sides, LANES), jnp.float32)
        gain_ref[1] = jnp.zeros((sides, LANES), jnp.float32)
        for _ in range(ITERS):

            def tile_normals(tile):
                left_real, left_imag, right_real, right_imag = columns(
                    [
                        gain_ref[0, pl.ds(tile, 1), :],
                        gain_ref[1, pl.ds(tile, 1), :],
                        gain_ref[0, pl.ds(tiles + tile, 1), :],
                        gain_ref[1, pl.ds(tiles + tile, 1), :],
                    ]
                )
                for slot, values in enumerate(
                    normals_of(
                        turned_ref[tile, 0],
                        turned_ref[tile, 1],
                        turned_ref[tile, 2],
                        right_real,
                        right_imag,
                        1,
                    )
                ):
                    normal_ref[slot, pl.ds(tile, 1), :] = values
                for slot, values in enumerate(
                    normals_of(
                        square_ref[tile, 0],
                        square_ref[tile, 1],
                        square_ref[tile, 2],
                        left_real,
                        left_imag,
                        -1,
                    )
                ):
                    normal_ref[slot, pl.ds(tiles + tile, 1), :] = values

            each(tiles, tile_normals)
            gain_real, gain_imag = gain_ref[0], gain_ref[1]
            below = shared_sum(normal_ref[2]) + LAMBDA
            gain_ref[0] = 0.5 * (
                gain_real + (shared_sum(normal_ref[0]) + LAMBDA * gain_real) / below
            )
            gain_ref[1] = 0.5 * (
                gain_imag + (shared_sum(normal_ref[1]) + LAMBDA * gain_imag) / below
            )
        final_ref[section] = gain_ref[...]


def residual_kernel(
    sections, times, dir_ref, vis_ref, model_ref, prior_ref, gain_ref, out_ref, factor_ref, column_ref
):
    for section in range(sections):
        rows = [gain_ref[0, section, k : k + 1, :] for k in range(4)]
        real, imag = outer_packed(
            rows[0], rows[1], both_halves(rows[2]), both_halves(rows[3]), column_ref
        )
        factor_ref[section, 0] = prior_ref[section, 0] - real
        factor_ref[section, 1] = prior_ref[section, 1] - imag

    def sample(time, carry):
        real = vis_ref[0, time, pl.ds(0, HALF, 2), :]
        imag = vis_ref[0, time, pl.ds(1, HALF, 2), :]
        for section in range(sections):
            model_real = model_ref[0, section, time, 0]
            model_imag = model_ref[0, section, time, 1]
            factor_real, factor_imag = factor_ref[section, 0], factor_ref[section, 1]
            real += factor_real * model_real - factor_imag * model_imag
            imag += factor_real * model_imag + factor_imag * model_real
        out_ref[0, time, pl.ds(0, HALF, 2), :] = real
        out_ref[0, time, pl.ds(1, HALF, 2), :] = imag
        return carry

    lax.fori_loop(0, times, sample, 0, unroll=4)


def on_device(
    visibilities,
    hour_angle,
    antenna_layout_coords,
    point_coords,
    point_flux,
    counts,
    peel_order,
    earlier_gain_amplitude,
    earlier_gain_phase,
    tile_blocks,
):
    sections, dirs = point_coords.shape[0], lax.axis_size("dir")
    pols, tiles = lax.axis_size("pol"), lax.axis_size("bl")
    group = dirs * pols
    comps = point_flux.shape[1]
    intervals, total_times = visibilities.shape[0], visibilities.shape[3]
    times = total_times // dirs
    me_dir = lax.axis_index("dir")
    assert group % intervals == 0 and group >= intervals

    vis = visibilities.reshape(intervals, total_times, 2, HALF, LANES)
    vis = vis.transpose(0, 1, 3, 2, 4).reshape(intervals, total_times, ABLK, LANES)
    place = me_dir[None].astype(jnp.int32)

    count = 3 * sections + sections * (sections - 1)
    rows = 8 + count * HALF
    whole = lambda shape: pl.BlockSpec(shape, lambda i, *s: (0,) * len(shape))
    vis_spec = pl.BlockSpec((1, times, ABLK, LANES), lambda i, *s: (i, s[0][0], 0, 0))
    model_spec = pl.BlockSpec(
        (1, sections, times, 2, HALF, LANES), lambda i, *s: (i, 0, 0, 0, 0, 0)
    )
    prior_shape = (sections, 2, HALF, LANES)
    limit = 62 * 1024 * 1024
    model, sums, prior = pl.pallas_call(
        functools.partial(model_kernel, sections, times, comps, 8),
        out_shape=(
            jax.ShapeDtypeStruct((intervals, sections, times, 2, HALF, LANES), jnp.float32),
            jax.ShapeDtypeStruct((intervals, rows, LANES), jnp.float32),
            jax.ShapeDtypeStruct(prior_shape, jnp.float32),
        ),
        grid_spec=pltpu.PrefetchScalarGridSpec(
            num_scalar_prefetch=4,
            grid=(intervals,),
            in_specs=[
                whole(antenna_layout_coords.shape),
                whole(point_coords.shape),
                whole(point_flux.shape),
                whole(earlier_gain_amplitude.shape),
                whole(earlier_gain_phase.shape),
                pl.BlockSpec((1, 1, total_times), lambda i, *s: (i, 0, 0)),
                vis_spec,
            ],
            out_specs=(
                model_spec,
                pl.BlockSpec((1, rows, LANES), lambda i, *s: (i, 0, 0)),
                whole(prior_shape),
            ),
            scratch_shapes=[
                pltpu.VMEM((4, ABLK, CHUNK), jnp.float32),
                pltpu.VMEM((sections, 1, comps), jnp.float32),
                pltpu.VMEM((2, ABLK, LANES), jnp.float32),
                pltpu.VMEM((sections, times, comps), jnp.float32),
                pltpu.VMEM((sections, times, comps), jnp.float32),
            ],
        ),
        compiler_params=pltpu.CompilerParams(vmem_limit_bytes=limit),
        name="models",
    )(
        place,
        peel_order,
        counts,
        tile_blocks,
        antenna_layout_coords,
        point_coords,
        point_flux,
        earlier_gain_amplitude,
        earlier_gain_phase,
        hour_angle,
        vis,
    )

    dma = pltpu.SemaphoreType.DMA
    gains = pl.pallas_call(
        functools.partial(solve_kernel, sections, intervals, tiles, dirs, pols),
        out_shape=jax.ShapeDtypeStruct((intervals, sections, 8, LANES), jnp.float32),
        in_specs=[pl.BlockSpec(memory_space=pl.ANY)],
        out_specs=pl.BlockSpec(memory_space=pltpu.VMEM),
        scratch_shapes=[
            pltpu.VMEM((group, rows, LANES), jnp.float32),
            pltpu.VMEM((tiles, rows, LANES), jnp.float32),
            pltpu.VMEM((tiles, sections, 8, LANES), jnp.float32),
            pltpu.VMEM((intervals, sections, 8, LANES), jnp.float32),
            pltpu.VMEM((tiles, 5, ABLK, LANES), jnp.float32),
            pltpu.VMEM((tiles, 3, ABLK, LANES), jnp.float32),
            pltpu.VMEM((2, 2 * tiles, LANES), jnp.float32),
            pltpu.VMEM((3, 2 * tiles, LANES), jnp.float32),
            pltpu.VMEM((sections, 2, 2 * tiles, LANES), jnp.float32),
            dma,
            dma((2, group - 1)),
            dma((2, group - 1)),
            dma((2,)),
            dma((2, tiles)),
            dma((tiles * group,)),
            dma((intervals,)),
        ],
        compiler_params=pltpu.CompilerParams(
            collective_id=0, has_side_effects=True, vmem_limit_bytes=62 * 1024 * 1024
        ),
        name="solve",
    )(sums)

    out = pl.pallas_call(
        functools.partial(residual_kernel, sections, times),
        out_shape=jax.ShapeDtypeStruct((intervals, times, ABLK, LANES), jnp.float32),
        grid_spec=pltpu.PrefetchScalarGridSpec(
            num_scalar_prefetch=1,
            grid=(intervals,),
            in_specs=[
                vis_spec,
                model_spec,
                whole(prior_shape),
                pl.BlockSpec((1, sections, 8, LANES), lambda i, *s: (i, 0, 0, 0)),
            ],
            out_specs=pl.BlockSpec((1, times, ABLK, LANES), lambda i, *s: (i, 0, 0, 0)),
            scratch_shapes=[
                pltpu.VMEM((sections, 2, HALF, LANES), jnp.float32),
                pltpu.VMEM((2, ABLK, LANES), jnp.float32),
            ],
        ),
        compiler_params=pltpu.CompilerParams(vmem_limit_bytes=limit),
        name="residual",
    )(place, vis, model, prior, gains)
    out = out.reshape(intervals, times, HALF, 2, LANES).transpose(0, 1, 3, 2, 4)
    return out.reshape(intervals, 1, 1, times, 2, HALF * LANES)


def solution(mesh):
    placed = (
        P("band", "bl", "pol", None, None, None),
        P(None, "pol", None),
        P(),
        P(),
        P(),
        P(),
        P(),
        P("band", None),
        P("band", None),
        P("bl", None),
    )
    return jax.shard_map(
        on_device,
        mesh=mesh,
        in_specs=placed,
        out_specs=P("band", "bl", "pol", "dir", None, None),
        check_vma=False,
    )
```
